128 devices in a mesh: prompt: 16 (over y, z), resp: 8 (over x, core).
Axes of the slice: x: 4, y: 4, z: 4, core: 2. Of those that a mesh axis runs over, the one named last changes fastest.
Arguments:
- queries: bfloat16 [16, 8, 16, 16, 5120], P('prompt', 'resp'), may hold values from -80 to 80
- grad_out: bfloat16 [16, 8, 16, 16, 5120], P('prompt', 'resp'), may hold values from -6 to 6
- response_keys: bfloat16 [16, 8, 16, 16, 1024], P('prompt', 'resp'), may hold values from -4 to 4
- response_values: bfloat16 [16, 8, 16, 16, 1024], P('prompt', 'resp'), may hold values from -6 to 6
- prompt_prefix_keys: bfloat16 [16, 384, 1024], P('prompt', 'resp'), may hold values from -6 to 6
- prompt_prefix_values: bfloat16 [16, 384, 1024], P('prompt', 'resp'), may hold values from -6 to 6
- lengths: int32 [16, 8, 16], P('prompt', 'resp'), may hold values from 1 to 16, 160 in all within a row
- prompt_of: int32 [16, 8, 16], P('prompt', 'resp'), may hold values from 0 to 15, each once within a row
Outputs:
- attn_out: bfloat16 [16, 8, 16, 16, 5120], P('prompt', 'resp')
- query_grads: bfloat16 [16, 8, 16, 16, 5120], P('prompt', 'resp')
- resp_key_grads: bfloat16 [16, 8, 16, 16, 1024], P('prompt', 'resp')
- resp_value_grads: bfloat16 [16, 8, 16, 16, 1024], P('prompt', 'resp')
- prefix_key_grads: float32 [16, 384, 1024], P('prompt', 'resp')
- prefix_value_grads: float32 [16, 384, 1024], P('prompt', 'resp')
The draws below stay inside these ranges and needn't reach their ends.
Inputs may be any that keep to these rules, and one draw needn't show every extreme that they name: `prompt_of`: on every device the 16 responses answer 16 different prompts. On every device the lengths sum to 160 and the longest is 16.
All inputs are finite; a program needn't handle non-finite values.
Results may differ from the reference program's by a relative error of at most 0.017.
Values may be sent and summed in bfloat16 or wider, within the bound.
A program may use at most 192 MiB of HBM per device.

```python
import math
import jax
import jax.numpy as jnp
import numpy as np
from jax import lax

NQH = 40
KEY_HEADS = 8
HEAD_WIDTH = 128
QUERY_PER_KEY = 5
RESPONSE_SLOTS = 16
PREFIX_LENGTH = 384
LIVE = 160
N_PROMPT = 16
N_RESP = 8


def shared_keys(key):
    return jnp.clip(jax.random.normal(key, (N_PROMPT, N_RESP, N_PROMPT, RESPONSE_SLOTS, KEY_HEADS * HEAD_WIDTH), jnp.float32), -4.0, 4.0)


def draw_response_keys(key, part):
    base = shared_keys(key)
    return base.astype(jnp.bfloat16)


def draw_queries(key, part):
    key = jax.random.fold_in(key, 23)
    tensor_layout = (N_PROMPT, N_RESP, N_PROMPT, RESPONSE_SLOTS, NQH * HEAD_WIDTH)
    return jnp.clip(jax.random.normal(key, tensor_layout, jnp.float32), -4.0, 4.0).astype(jnp.bfloat16)


def level_of(rng, extent, cuts, smallest, high):
    gain = 1.0
    for dim, shards_of in cuts:
        steps = jax.random.uniform(jax.random.fold_in(jax.random.fold_in(rng, 6), dim), (shards_of,), jnp.float32, smallest / len(cuts), high / len(cuts))
        gain = gain * jnp.repeat(jnp.exp(steps), extent[dim] // shards_of).reshape((-1,) + (1,) * (len(extent) - 1 - dim))
    return gain


def profile(amount, total, reach, slope):
    portions = [(1 << 20) // math.isqrt(grade ** slope) + 1 for grade in range(2, amount + 1)]
    surplus, counts = total - reach - (amount - 1), [1] * (amount - 1)
    while surplus > 0:
        free = [i for i in range(amount - 1) if counts[i] < reach]
        pool, budget = sum([portions[i] for i in free]), surplus
        for i in free:
            addition = min(reach - counts[i], max(1, budget * portions[i] // pool), surplus)
            counts[i] = counts[i] + addition
            surplus = surplus - addition
    return np.array([reach] + counts)


def uneven(own_key, amount, total, limit, skew):
    if amount == 2:
        one = jax.random.randint(own_key, (), max(1, total - limit), min(limit, total - 1) + 1)
        return jnp.stack([one, total - one])
    sizes = jnp.asarray(profile(amount, total, limit, skew), jnp.int32)
    couples = (amount - 1) // 2
    source_of, receiver = sizes[1:1 + 2 * couples:2], sizes[2:2 + 2 * couples:2]
    slack = jnp.minimum(source_of - 1, limit - receiver)
    moved = jax.random.randint(jax.random.fold_in(own_key, 1), (couples,), 0, 1 << 20) % (slack + 1)
    sizes = sizes.at[1:1 + 2 * couples:2].set(source_of - moved).at[2:2 + 2 * couples:2].set(receiver + moved)
    return sizes[jax.random.permutation(jax.random.fold_in(own_key, 2), amount)]


def bell_draw(rng, shape, scale, limit, cuts=(), held_as=jnp.bfloat16):
    drawn = scale * jax.random.normal(rng, shape, jnp.float32)
    if cuts:
        drawn = drawn * level_of(rng, shape, cuts, -0.22, 0.18)
    return jnp.clip(drawn, -limit, limit).astype(held_as)


def setup_inputs(seed: int = 0) -> dict:
    key_of = jax.random.split(jax.random.key(seed), 9)
    return {
        "queries": draw_queries(jax.random.fold_in(key_of[8], 71), 0),
        "grad_out": bell_draw(key_of[1], (N_PROMPT, N_RESP, N_PROMPT, RESPONSE_SLOTS, NQH * HEAD_WIDTH), 1.0, 6.0, ((0, 16), (1, 8))),
        "response_keys": draw_response_keys(jax.random.fold_in(key_of[8], 71), 0),
        "response_values": bell_draw(key_of[3], (N_PROMPT, N_RESP, N_PROMPT, RESPONSE_SLOTS, KEY_HEADS * HEAD_WIDTH), 1.0, 6.0, ((0, 16), (1, 8))),
        "prompt_prefix_keys": bell_draw(key_of[4], (N_PROMPT, PREFIX_LENGTH, KEY_HEADS * HEAD_WIDTH), 1.0, 6.0, ((0, 16), (1, 8))),
        "prompt_prefix_values": bell_draw(key_of[5], (N_PROMPT, PREFIX_LENGTH, KEY_HEADS * HEAD_WIDTH), 1.0, 6.0, ((0, 16), (1, 8))),
        "lengths": jax.vmap(lambda own: uneven(own, N_PROMPT, LIVE, RESPONSE_SLOTS, 2))(jax.random.split(key_of[6], N_PROMPT * N_RESP)).reshape((N_PROMPT, N_RESP, N_PROMPT)).astype(jnp.int32),
        "prompt_of": jax.vmap(lambda own: jax.random.permutation(own, N_PROMPT))(jax.random.split(key_of[7], N_PROMPT * N_RESP)).reshape((N_PROMPT, N_RESP, N_PROMPT)).astype(jnp.int32),
    }


def as_float(values):
    return values.astype(jnp.float32)


def rounded(values):
    return as_float(lax.optimization_barrier(values.astype(jnp.bfloat16)))


def prefix_forward(queries, key_rows, value_rows):
    row_count = queries.shape[0]
    factor = HEAD_WIDTH ** -0.5
    outputs = []
    totals = []
    for key_value_head in range(KEY_HEADS):
        query_part = as_float(queries[:, key_value_head * QUERY_PER_KEY * HEAD_WIDTH:(key_value_head + 1) * QUERY_PER_KEY * HEAD_WIDTH]).reshape(row_count, QUERY_PER_KEY, HEAD_WIDTH)
        key_part = as_float(key_rows[:, key_value_head * HEAD_WIDTH:(key_value_head + 1) * HEAD_WIDTH])
        value_part = as_float(value_rows[:, key_value_head * HEAD_WIDTH:(key_value_head + 1) * HEAD_WIDTH])
        scores = jnp.einsum("rgd,kd->rgk", query_part, key_part) * factor
        largest = jnp.max(scores, axis=-1)
        weights = jnp.exp(scores - largest[..., None])
        summed = jnp.sum(weights, axis=-1)
        mixture = jnp.einsum("rgk,kd->rgd", rounded(weights), value_part) / summed[..., None]
        outputs.append(mixture.reshape(row_count, QUERY_PER_KEY * HEAD_WIDTH))
        totals.append(largest + jnp.log(summed))
    return jnp.concatenate(outputs, axis=1), jnp.concatenate(totals, axis=1)


def causal_mask(row_extent):
    return lax.broadcasted_iota(jnp.int32, (row_extent, row_extent), 0) >= lax.broadcasted_iota(jnp.int32, (row_extent, row_extent), 1)


def self_forward(queries, key_rows, value_rows):
    batch_size, row_extent = queries.shape[0], queries.shape[1]
    causal = causal_mask(row_extent)
    factor = HEAD_WIDTH ** -0.5
    outputs = []
    totals = []
    for key_value_head in range(KEY_HEADS):
        query_part = as_float(queries[..., key_value_head * QUERY_PER_KEY * HEAD_WIDTH:(key_value_head + 1) * QUERY_PER_KEY * HEAD_WIDTH]).reshape(batch_size, row_extent, QUERY_PER_KEY, HEAD_WIDTH)
        key_part = as_float(key_rows[..., key_value_head * HEAD_WIDTH:(key_value_head + 1) * HEAD_WIDTH])
        value_part = as_float(value_rows[..., key_value_head * HEAD_WIDTH:(key_value_head + 1) * HEAD_WIDTH])
        scores = jnp.einsum("btgd,bsd->btgs", query_part, key_part) * factor
        scores = jnp.where(causal[None, :, None, :], scores, -jnp.inf)
        largest = jnp.max(scores, axis=-1)
        weights = jnp.exp(scores - largest[..., None])
        summed = jnp.sum(weights, axis=-1)
        mixture = jnp.einsum("btgs,bsd->btgd", rounded(weights), value_part) / summed[..., None]
        outputs.append(mixture.reshape(batch_size, row_extent, QUERY_PER_KEY * HEAD_WIDTH))
        totals.append(largest + jnp.log(summed))
    return jnp.concatenate(outputs, axis=2), jnp.concatenate(totals, axis=2)


def merge_parts(out_prefix, total_prefix, out_self, total_self):
    row_count = out_prefix.shape[0]
    highest = jnp.maximum(total_prefix, total_self)
    log_total = highest + jnp.log(jnp.exp(total_prefix - highest) + jnp.exp(total_self - highest))
    share_prefix = jnp.exp(total_prefix - log_total)[..., None]
    share_self = jnp.exp(total_self - log_total)[..., None]
    merged = share_prefix * out_prefix.reshape(row_count, NQH, HEAD_WIDTH) + share_self * as_float(out_self).reshape(row_count, NQH, HEAD_WIDTH)
    return merged.reshape(row_count, NQH * HEAD_WIDTH), log_total


def prefix_backward(queries, grads, log_total, row_dot, key_rows, value_rows):
    row_count = queries.shape[0]
    factor = HEAD_WIDTH ** -0.5
    query_grads, key_grads, value_grads = [], [], []
    for key_value_head in range(KEY_HEADS):
        low, high = key_value_head * QUERY_PER_KEY, (key_value_head + 1) * QUERY_PER_KEY
        query_part = as_float(queries[:, low * HEAD_WIDTH:high * HEAD_WIDTH]).reshape(row_count, QUERY_PER_KEY, HEAD_WIDTH)
        grad_part = as_float(grads[:, low * HEAD_WIDTH:high * HEAD_WIDTH]).reshape(row_count, QUERY_PER_KEY, HEAD_WIDTH)
        key_part = as_float(key_rows[:, key_value_head * HEAD_WIDTH:(key_value_head + 1) * HEAD_WIDTH])
        value_part = as_float(value_rows[:, key_value_head * HEAD_WIDTH:(key_value_head + 1) * HEAD_WIDTH])
        scores = jnp.einsum("rgd,kd->rgk", query_part, key_part) * factor
        weights = jnp.exp(scores - log_total[:, low:high, None])
        weight_grad = jnp.einsum("rgd,kd->rgk", grad_part, value_part)
        score_grad = weights * (weight_grad - row_dot[:, low:high, None])
        value_grads.append(jnp.einsum("rgk,rgd->kd", rounded(weights), grad_part))
        key_grads.append(jnp.einsum("rgk,rgd->kd", rounded(score_grad), query_part) * factor)
        query_grads.append((jnp.einsum("rgk,kd->rgd", rounded(score_grad), key_part) * factor).reshape(row_count, QUERY_PER_KEY * HEAD_WIDTH))
    return jnp.concatenate(query_grads, axis=1), jnp.concatenate(key_grads, axis=1), jnp.concatenate(value_grads, axis=1)


def self_backward(queries, grads, log_total, row_dot, key_rows, value_rows):
    batch_size, row_extent = queries.shape[0], queries.shape[1]
    causal = causal_mask(row_extent)
    factor = HEAD_WIDTH ** -0.5
    query_grads, key_grads, value_grads = [], [], []
    for key_value_head in range(KEY_HEADS):
        low, high = key_value_head * QUERY_PER_KEY, (key_value_head + 1) * QUERY_PER_KEY
        query_part = as_float(queries[..., low * HEAD_WIDTH:high * HEAD_WIDTH]).reshape(batch_size, row_extent, QUERY_PER_KEY, HEAD_WIDTH)
        grad_part = as_float(grads[..., low * HEAD_WIDTH:high * HEAD_WIDTH]).reshape(batch_size, row_extent, QUERY_PER_KEY, HEAD_WIDTH)
        key_part = as_float(key_rows[..., key_value_head * HEAD_WIDTH:(key_value_head + 1) * HEAD_WIDTH])
        value_part = as_float(value_rows[..., key_value_head * HEAD_WIDTH:(key_value_head + 1) * HEAD_WIDTH])
        scores = jnp.einsum("btgd,bsd->btgs", query_part, key_part) * factor
        scores = jnp.where(causal[None, :, None, :], scores, -jnp.inf)
        weights = jnp.exp(scores - log_total[:, :, low:high, None])
        weight_grad = jnp.einsum("btgd,bsd->btgs", grad_part, value_part)
        score_grad = weights * (weight_grad - row_dot[:, :, low:high, None])
        value_grads.append(jnp.einsum("btgs,btgd->bsd", rounded(weights), grad_part))
        key_grads.append(jnp.einsum("btgs,btgd->bsd", rounded(score_grad), query_part) * factor)
        query_grads.append((jnp.einsum("btgs,bsd->btgd", rounded(score_grad), key_part) * factor).reshape(batch_size, row_extent, QUERY_PER_KEY * HEAD_WIDTH))
    return jnp.concatenate(query_grads, axis=2), jnp.concatenate(key_grads, axis=2), jnp.concatenate(value_grads, axis=2)


def reference(queries, grad_out, response_keys, response_values, prompt_prefix_keys, prompt_prefix_values, lengths, prompt_of):
    leading = queries.shape[:3]
    valid = jnp.arange(RESPONSE_SLOTS, dtype=jnp.int32)[None, None, None, :] < lengths[..., None]
    masked_grad = jnp.where(valid[..., None], grad_out, jnp.zeros((), grad_out.dtype))

    def flatten(values):
        return values.reshape((-1, RESPONSE_SLOTS, values.shape[-1]))

    def unflatten(values):
        return values.reshape(leading + values.shape[1:])

    self_out, self_total = self_forward(flatten(queries), flatten(response_keys), flatten(response_values))
    self_out = lax.optimization_barrier(self_out.astype(jnp.bfloat16))
    self_out = unflatten(self_out)
    self_total = unflatten(self_total)
    slot_ids = jnp.arange(N_PROMPT, dtype=jnp.int32)
    matches = prompt_of[..., None, :] == slot_ids[:, None]
    senders = jnp.sum(jnp.where(matches, slot_ids[None, :], 0), axis=-1).astype(jnp.int32)

    def to_prompts(values):
        picked = jnp.take_along_axis(values, senders[..., None, None], axis=2)
        return jnp.moveaxis(picked, 2, 0)

    def per_prompt(items):
        query_g, grad_g, out_g, total_g, key_g, value_g = items

        def rows(values):
            return values.reshape((-1, values.shape[-1]))

        def back_shape(values):
            return values.reshape(query_g.shape[:-1] + (values.shape[-1],))

        prefix_out, prefix_total = prefix_forward(rows(query_g), key_g, value_g)
        merged, log_total = merge_parts(prefix_out, prefix_total, rows(out_g), rows(total_g))
        row_dot = jnp.sum((as_float(rows(grad_g)) * merged).reshape(-1, NQH, HEAD_WIDTH), axis=2)
        query_grad, key_grad, value_grad = prefix_backward(rows(query_g), rows(grad_g), log_total, row_dot, key_g, value_g)
        results = (back_shape(merged.astype(jnp.bfloat16)), back_shape(lax.optimization_barrier(query_grad.astype(jnp.bfloat16))), back_shape(log_total), back_shape(row_dot))
        return results, key_grad, value_grad

    results, prefix_key_grads, prefix_value_grads = lax.map(per_prompt, (to_prompts(queries), to_prompts(masked_grad), to_prompts(self_out), to_prompts(self_total), prompt_prefix_keys, prompt_prefix_values))

    def to_home(values):
        moved = jnp.moveaxis(values, 0, 2)
        return jnp.take_along_axis(moved, prompt_of[..., None, None], axis=2)

    home_out, home_query, home_total, home_dot = [to_home(item) for item in results]
    self_query, self_key, self_value = self_backward(flatten(queries), flatten(masked_grad), flatten(home_total), flatten(home_dot), flatten(response_keys), flatten(response_values))
    attn_out = jnp.where(valid[..., None], home_out, jnp.zeros((), home_out.dtype))
    query_grads = (as_float(home_query) + unflatten(self_query)).astype(jnp.bfloat16)
    return attn_out, query_grads, unflatten(self_key).astype(jnp.bfloat16), unflatten(self_value).astype(jnp.bfloat16), prefix_key_grads, prefix_value_grads
```

```python
import jax
import jax.numpy as jnp
from jax import lax
from jax.experimental import pallas as pl
from jax.experimental.pallas import tpu as pltpu
from jax.sharding import PartitionSpec as P

KEY_HEADS = 8
WIDTH = 128
GROUP = 5
SLOTS = 16
RESPONSES = 16
TOKENS = SLOTS * RESPONSES
LIVE = 160
PREFIX = 384
SIDE = 4
ROWS = PREFIX // 8
PIECE = 2 * PREFIX
GW = GROUP * WIDTH
MSG = 2 * GW + 2 * WIDTH
MESH = pl.DeviceIdType.MESH
BF16 = jnp.bfloat16
F32 = jnp.float32
SCALE = WIDTH**-0.5
EXP2_SCALE = SCALE * 1.4426950408889634
VMEM_LIMIT = 58 * 1024 * 1024


class Place:
    def __init__(self):
        prompt, resp = lax.axis_index("prompt"), lax.axis_index("resp")
        self.y, self.z = prompt // SIDE, prompt % SIDE
        self.x, self.c = resp // 2, resp % 2
        self.prompt, self.resp = prompt, resp
        x, y, z, c = self.x, self.y, self.z, self.c
        self.sibling = (prompt, x * 2 + 1 - c)
        self.home_slot = 2 * (x * (1 - c) + y * c) + c
        self.head = x * (1 - c) + (SIDE + y) * c
        self.line = y * (1 - c) + x * c
        self.routes = []
        for k in (2, 1, 3):
            xd, yd = (x + k) % SIDE, (y + k) % SIDE
            self.routes.append((xd, 2 * x + c, (prompt, 2 * xd)))
            self.routes.append((SIDE + yd, 2 * y + c, (yd * SIDE + z, 2 * x + 1)))
        self.routes.append(((SIDE + y) * (1 - c) + x * c, 2 * y * (1 - c) + (2 * x + 1) * c, self.sibling))
        self.routes.append((self.head, self.home_slot, None))

    def source(self, k, core):
        along = (self.x * (1 - self.c) + self.y * self.c + k) % SIDE
        prompt = self.prompt * (1 - self.c) + (along * SIDE + self.z) * self.c
        resp = (along * 2 + core) * (1 - self.c) + (2 * self.x + core) * self.c
        return 2 * along + core, (prompt, resp)

    def line_peer(self, k):
        prompt = ((self.y + k * (1 - self.c)) % SIDE) * SIDE + self.z
        return (prompt, ((self.x + k * self.c) % SIDE) * 2 + self.c)

    def z_peer(self, k):
        return (self.y * SIDE + (self.z + k) % SIDE, self.resp)

    def barrier(self):
        sem = pltpu.get_barrier_semaphore()
        peers = [self.sibling]
        for k in (1, 2, 3):
            peers.append(self.z_peer(k))
            for core in (0, 1):
                peers.append((self.prompt, ((self.x + k) % SIDE) * 2 + core))
                peers.append((((self.y + k) % SIDE) * SIDE + self.z, 2 * self.x + core))
        for peer in peers:
            pl.semaphore_signal(sem, inc=1, device_id=peer, device_id_type=MESH)
        pl.semaphore_wait(sem, len(peers))


def remote(src, dst, send, recv, device):
    return pltpu.make_async_remote_copy(
        src_ref=src, dst_ref=dst, send_sem=send, recv_sem=recv, device_id=device, device_id_type=MESH
    )


def pack_rows(len_ref, prm_ref):
    lane = lax.broadcasted_iota(jnp.int32, (1, TOKENS), 1)
    response, token = lane >> 4, lane & (SLOTS - 1)
    row = jnp.full((1, TOKENS), -1, jnp.int32)
    slot = jnp.zeros((1, TOKENS), jnp.int32)
    start = jnp.int32(0)
    for j in range(RESPONSES):
        length = len_ref[j]
        mine = response == j
        row = jnp.where(mine & (token < length), start + token, row)
        slot = jnp.where(mine, prm_ref[j] * SLOTS + token, slot)
        start = start + length
    return row, slot


def one_hot_pack(row):
    packed = lax.broadcasted_iota(jnp.int32, (LIVE, TOKENS), 0)
    return jnp.where(packed == row, 1.0, 0.0).astype(BF16)


def dot(a, b, dims):
    return lax.dot_general(a, b, (dims, ((), ())), preferred_element_type=F32)


NN = ((1,), (0,))
NT = ((1,), (1,))
TN = ((0,), (0,))


def scatter_kernel(
    len_ref, prm_ref, q, g, k, v, pk, pv, recv, slots, kv,
    xb, send, slot_send, in_sem, x_send, x_recv, sl_send, sl_recv, a_send, a_recv, b_send, b_recv, c_send, c_recv, own_sem,
):
    me = Place()
    routes = me.routes
    for n, (head, _, _) in enumerate(routes):
        wide = pl.ds(pl.multiple_of(head * GW, WIDTH), GW)
        narrow = pl.ds(pl.multiple_of(head * WIDTH, WIDTH), WIDTH)
        for src, cols, low, size in ((q, wide, 0, GW), (g, wide, GW, GW), (k, narrow, 2 * GW, WIDTH), (v, narrow, 2 * GW + WIDTH, WIDTH)):
            pltpu.make_async_copy(src.at[:, cols], xb.at[n, :, pl.ds(low, size)], in_sem.at[n]).start()
    me.barrier()

    stage_a = []
    for n, (head, _, device) in enumerate(routes):
        narrow = pl.ds(pl.multiple_of(head * WIDTH, WIDTH), WIDTH)
        on_y = head // SIDE
        for i, src in enumerate((pk, pv)):
            piece = me.y * (1 - on_y) + me.x * on_y
            low = (i * PREFIX + me.resp * ROWS) * (1 - on_y) + ((me.y * 2 + i) * 2 * ROWS + me.c * ROWS) * on_y
            dst = kv.at[me.z, piece, pl.ds(pl.multiple_of(low, 16), ROWS)]
            slot = routes[n][1]
            if device is None:
                copy = pltpu.make_async_copy(src.at[:, narrow], dst, own_sem.at[1 + i])
            else:
                copy = remote(src.at[:, narrow], dst, a_send.at[n, i], a_recv.at[slot, i], device)
            copy.start()
            stage_a.append(copy)

    row, slot = pack_rows(len_ref, prm_ref)
    pack = one_hot_pack(row)
    slot8 = jnp.broadcast_to(slot, (8, TOKENS)).astype(F32).astype(BF16)
    slot_send[...] = dot(slot8, pack, NT)
    sent = []
    for n, (_, there, device) in enumerate(routes):
        if device is None:
            copy = pltpu.make_async_copy(slot_send, slots.at[there], own_sem.at[3])
        else:
            copy = remote(slot_send, slots.at[there], sl_send.at[n], sl_recv.at[there], device)
        copy.start()
        sent.append(copy)

    def pack_and_send(n):
        _, there, device = routes[n]
        pltpu.make_async_copy(xb.at[n], xb.at[n], in_sem.at[n]).wait()
        send[n] = dot(pack, xb[n], NN).astype(BF16)
        if device is None:
            copy = pltpu.make_async_copy(send.at[n], recv.at[there], own_sem.at[0])
        else:
            copy = remote(send.at[n], recv.at[there], x_send.at[n], x_recv.at[there], device)
        copy.start()
        sent.append(copy)

    def spread(piece, index):
        for k in (2, 1, 3):
            ref = kv.at[me.z, piece]
            copy = remote(ref, ref, c_send.at[index, k - 1], c_recv.at[index, k - 1], me.z_peer(k))
            copy.start()
            sent.append(copy)

    pack_and_send(0)
    pack_and_send(1)
    for k in range(SIDE):
        for core in (0, 1):
            there, device = me.source(k, core)
            sx = (me.x + k) % SIDE * (1 - me.c) + me.x * me.c
            sy = me.y * (1 - me.c) + (me.y + k) % SIDE * me.c
            piece = sy * (1 - me.c) + sx * me.c
            for i in (0, 1):
                low = (i * PREFIX + (2 * sx + core) * ROWS) * (1 - me.c) + ((sy * 2 + i) * 2 * ROWS + core * ROWS) * me.c
                dst = kv.at[me.z, piece, pl.ds(pl.multiple_of(low, 16), ROWS)]
                wait = remote(dst, dst, a_send.at[0, i], a_recv.at[there, i], me.sibling)
                if k == 0:

                    @pl.when(me.c != core)
                    def _():
                        wait.wait_recv()
                else:
                    wait.wait_recv()
    stage_a[-2].wait()
    stage_a[-1].wait()
    for k in (2, 1, 3):
        ref = kv.at[me.z, me.line]
        copy = remote(ref, ref, b_send.at[k - 1], b_recv.at[k - 1], me.line_peer(k))
        copy.start()
        sent.append(copy)
    spread(me.line, 0)
    for n in range(2, 8):
        pack_and_send(n)
    for k in (1, 3, 2):
        piece = (me.line + k) % SIDE
        ref = kv.at[me.z, piece]
        remote(ref, ref, b_send.at[0], b_recv.at[SIDE - k - 1], me.sibling).wait_recv()
        spread(piece, SIDE - k)
    for k in (1, 3, 2):
        for index in range(SIDE):
            ref = kv.at[(me.z + k) % SIDE, (me.line + SIDE - index) % SIDE]
            remote(ref, ref, c_send.at[0, 0], c_recv.at[index, SIDE - k - 1], me.sibling).wait_recv()
    for k in range(SIDE):
        for core in (0, 1):
            there, device = me.source(k, core)

            def arrived(there=there):
                remote(recv.at[there], recv.at[there], x_send.at[0], x_recv.at[there], me.sibling).wait_recv()
                remote(slots.at[there], slots.at[there], sl_send.at[0], sl_recv.at[there], me.sibling).wait_recv()

            if k == 0:
                pl.when(me.c != core)(arrived)
            else:
                arrived()
    for copy in stage_a[:-2] + sent:
        if isinstance_remote(copy):
            copy.wait_send()
        else:
            copy.wait()


def isinstance_remote(copy):
    return copy.is_remote if hasattr(copy, "is_remote") else copy.device_id is not None


def attention_kernel(recv, slots, kv, ret, dkv, xu, ou):
    c = lax.axis_index("resp") % 2

    def one_hot(i):
        slot = slots[i][0:1, :LIVE].astype(jnp.int32)
        return jnp.where(lax.broadcasted_iota(jnp.int32, (TOKENS, LIVE), 0) == slot, 1.0, 0.0).astype(BF16)

    def unpack(i, carry):
        rows = dot(one_hot(i), recv[i], NN).astype(BF16)
        xu[:, pl.ds(pl.multiple_of(i * SLOTS, SLOTS), SLOTS), :] = rows.reshape(RESPONSES, SLOTS, MSG)
        return carry

    lax.fori_loop(0, 8, unpack, 0)

    own_rows = lax.broadcasted_iota(jnp.int32, (WIDTH, WIDTH), 0)
    own_cols = lax.broadcasted_iota(jnp.int32, (WIDTH, WIDTH), 1)
    own_mask = (own_rows >> 4 == own_cols >> 4) & (own_cols <= own_rows)
    own_mask = jnp.concatenate([own_mask] * GROUP, axis=0)

    def prompt(g, carry):
        gy, gz = g // SIDE, g % SIDE

        def chunk(i, quarter):
            piece = gy * (1 - c) + quarter * c
            low = (i * PREFIX + quarter * 96) * (1 - c) + (gy * 2 + i) * 96 * c
            return gz, piece, pl.ds(pl.multiple_of(low, 16), 96)

        def heads(low):
            return jnp.concatenate([xu[g, :, low + a * WIDTH : low + (a + 1) * WIDTH] for a in range(GROUP)], axis=0)

        queries, grads = heads(0), heads(GW)
        keys = jnp.concatenate([kv[chunk(0, i)] for i in range(SIDE)] + [xu[g, :, 2 * GW : 2 * GW + WIDTH]], axis=0)
        values = jnp.concatenate([kv[chunk(1, i)] for i in range(SIDE)] + [xu[g, :, 2 * GW + WIDTH :]], axis=0)
        scores = dot(queries, keys, NT)
        scores = jnp.concatenate(
            [scores[:, :PREFIX], jnp.where(own_mask, scores[:, PREFIX:], -1e30)], axis=1
        )
        top = jnp.max(scores, axis=1, keepdims=True)
        weights = jnp.exp2((scores - top) * EXP2_SCALE)
        total = jnp.sum(weights, axis=1, keepdims=True)
        over = 1.0 / total
        half = weights.astype(BF16)
        out = dot(half, values, NN) * over
        scaled = (grads.astype(F32) * over).astype(BF16)
        row_dot = jnp.sum(scaled.astype(F32) * out, axis=1, keepdims=True)
        score_grad = (weights * (dot(scaled, values, NT) - row_dot)).astype(BF16)
        query_grad = dot(score_grad, keys, NN) * SCALE
        key_grad = (dot(score_grad, queries, TN) * SCALE).astype(BF16)
        value_grad = dot(half, scaled, TN).astype(BF16)
        for i, rows in enumerate((key_grad, value_grad)):
            for quarter in range(SIDE):
                dkv[chunk(i, quarter)] = rows[quarter * 96 : (quarter + 1) * 96]
        for a in range(GROUP):
            ou[g, :, a * WIDTH : (a + 1) * WIDTH] = out[a * WIDTH : (a + 1) * WIDTH].astype(BF16)
            ou[g, :, GW + a * WIDTH : GW + (a + 1) * WIDTH] = query_grad[a * WIDTH : (a + 1) * WIDTH].astype(BF16)
        ou[g, :, 2 * GW : 2 * GW + WIDTH] = key_grad[PREFIX:]
        ou[g, :, 2 * GW + WIDTH :] = value_grad[PREFIX:]
        return carry

    lax.fori_loop(0, RESPONSES, prompt, 0)

    def repack(i, carry):
        rows = ou[:, pl.ds(pl.multiple_of(i * SLOTS, SLOTS), SLOTS), :].reshape(TOKENS, MSG)
        ret[i] = dot(one_hot(i), rows, TN).astype(BF16)
        return carry

    lax.fori_loop(0, 8, repack, 0)


def return_kernel(
    ret, dkv, back, grads,
    own, got_c, sum_c, got_b, final, in_sem, r_send, r_recv, c_send, c_recv, b_send, b_recv, a_send, a_recv, own_sem,
):
    me = Place()
    load = pltpu.make_async_copy(dkv.at[me.z], own, in_sem)
    load.start()
    me.barrier()
    sent = []
    for step, offset in enumerate((0, 1, 3, 2)):
        piece = (me.line + offset) % SIDE
        for k in (2, 1, 3):
            copy = remote(dkv.at[(me.z + k) % SIDE, piece], got_c.at[k - 1, piece], c_send.at[step, k - 1], c_recv.at[step, k - 1], me.z_peer(k))
            copy.start()
            sent.append(copy)
    local = []
    for k in (2, 1, 3, 0):
        for core in (0, 1):
            there, device = me.source(k, core)
            index = 2 * k + core
            if k == 0:

                @pl.when(me.c == core)
                def _():
                    pltpu.make_async_copy(ret.at[there], back.at[me.head], own_sem.at[0]).start()

                @pl.when(me.c != core)
                def _():
                    remote(ret.at[there], back.at[me.head], r_send.at[index], r_recv.at[me.head], device).start()
            else:
                copy = remote(ret.at[there], back.at[me.head], r_send.at[index], r_recv.at[me.head], device)
                copy.start()
                sent.append(copy)
    load.wait()
    for step, offset in enumerate((0, 1, 3, 2)):
        piece = (me.line + offset) % SIDE
        for k in (1, 3, 2):
            ref = got_c.at[k - 1, piece]
            remote(ref, ref, c_send.at[0, 0], c_recv.at[step, k - 1], me.sibling).wait_recv()
        total = own[piece].astype(F32) + got_c[0, piece].astype(F32) + got_c[1, piece].astype(F32) + got_c[2, piece].astype(F32)
        if offset == 0:
            final[...] = total
        else:
            sum_c[offset - 1] = total.astype(BF16)
            copy = remote(sum_c.at[offset - 1], got_b.at[offset - 1], b_send.at[offset - 1], b_recv.at[offset - 1], me.line_peer(offset))
            copy.start()
            sent.append(copy)
    for k in (1, 3, 2):
        ref = got_b.at[k - 1]
        remote(ref, ref, b_send.at[0], b_recv.at[k - 1], me.sibling).wait_recv()
    total = final[...] + got_b[0].astype(F32) + got_b[1].astype(F32) + got_b[2].astype(F32)
    sum_c[3] = total.astype(BF16)
    for k in (2, 1, 3, 0):
        for core in (0, 1):
            there, device = me.source(k, core)
            index = 2 * k + core
            sx = (me.x + k) % SIDE * (1 - me.c) + me.x * me.c
            sy = me.y * (1 - me.c) + (me.y + k) % SIDE * me.c
            for i in (0, 1):
                low = (i * PREFIX + (2 * sx + core) * ROWS) * (1 - me.c) + ((sy * 2 + i) * 2 * ROWS + core * ROWS) * me.c
                src = sum_c.at[3, pl.ds(pl.multiple_of(low, 16), ROWS)]
                dst = grads.at[me.head, i]
                if k == 0:

                    @pl.when(me.c == core)
                    def _():
                        pltpu.make_async_copy(src, dst, own_sem.at[1 + i]).start()

                    @pl.when(me.c != core)
                    def _():
                        remote(src, dst, a_send.at[index, i], a_recv.at[me.head, i], device).start()
                else:
                    copy = remote(src, dst, a_send.at[index, i], a_recv.at[me.head, i], device)
                    copy.start()
                    sent.append(copy)
    for head, _, device in me.routes:
        if device is None:
            pltpu.make_async_copy(back.at[head], back.at[head], own_sem.at[0]).wait()
            for i in (0, 1):
                pltpu.make_async_copy(grads.at[head, i], grads.at[head, i], own_sem.at[1 + i]).wait()
        else:
            remote(back.at[head], back.at[head], r_send.at[0], r_recv.at[head], me.sibling).wait_recv()
            for i in (0, 1):
                remote(grads.at[head, i], grads.at[head, i], a_send.at[0, i], a_recv.at[head, i], me.sibling).wait_recv()
    for copy in sent:
        copy.wait_send()
    for core in (0, 1):

        @pl.when(me.c != core)
        def _():
            there, device = me.source(0, core)
            remote(ret.at[there], back.at[me.head], r_send.at[core], r_recv.at[me.head], device).wait_send()
            for i in (0, 1):
                ref = sum_c.at[3, pl.ds(0, ROWS)]
                remote(ref, grads.at[me.head, i], a_send.at[core, i], a_recv.at[me.head, i], device).wait_send()


def unpack_kernel(len_ref, prm_ref, back, grads, attn, query, key, value, prefix_key, prefix_value, pack):
    @pl.when(pl.program_id(0) == 0)
    def _():
        row, _ = pack_rows(len_ref, prm_ref)
        pack[...] = one_hot_pack(row)

    rows = dot(pack[...], back[0], TN).astype(BF16)
    attn[...] = rows[:, :GW]
    query[...] = rows[:, GW : 2 * GW]
    key[...] = rows[:, 2 * GW : 2 * GW + WIDTH]
    value[...] = rows[:, 2 * GW + WIDTH :]
    prefix_key[...] = grads[0, 0].astype(F32)
    prefix_value[...] = grads[0, 1].astype(F32)


def spec(space):
    return pl.BlockSpec(memory_space=space)


DMA = pltpu.SemaphoreType.DMA


def local(queries, grad_out, response_keys, response_values, prompt_prefix_keys, prompt_prefix_values, lengths, prompt_of):
    q, g = queries.reshape(TOKENS, KEY_HEADS * GW), grad_out.reshape(TOKENS, KEY_HEADS * GW)
    k, v = response_keys.reshape(TOKENS, KEY_HEADS * WIDTH), response_values.reshape(TOKENS, KEY_HEADS * WIDTH)
    pk, pv = prompt_prefix_keys.reshape(ROWS, KEY_HEADS * WIDTH), prompt_prefix_values.reshape(ROWS, KEY_HEADS * WIDTH)
    lens, prompts = lengths.reshape(RESPONSES), prompt_of.reshape(RESPONSES)
    recv, slots, kv = pl.pallas_call(
        scatter_kernel,
        out_shape=(
            jax.ShapeDtypeStruct((8, LIVE, MSG), BF16),
            jax.ShapeDtypeStruct((8, 8, LIVE), F32),
            jax.ShapeDtypeStruct((SIDE, SIDE, PIECE, WIDTH), BF16),
        ),
        in_specs=[spec(pltpu.SMEM)] * 2 + [spec(pl.ANY)] * 6,
        out_specs=(spec(pl.ANY),) * 3,
        scratch_shapes=[
            pltpu.VMEM((8, TOKENS, MSG), BF16),
            pltpu.VMEM((8, LIVE, MSG), BF16),
            pltpu.VMEM((8, LIVE), F32),
            DMA((8,)), DMA((8,)), DMA((8,)), DMA((8,)), DMA((8,)), DMA((8, 2)), DMA((8, 2)),
            DMA((3,)), DMA((3,)), DMA((4, 3)), DMA((4, 3)), DMA((4,)),
        ],
        compiler_params=pltpu.CompilerParams(collective_id=0, has_side_effects=True, vmem_limit_bytes=VMEM_LIMIT),
    )(lens, prompts, q, g, k, v, pk, pv)
    ret, dkv = pl.pallas_call(
        attention_kernel,
        out_shape=(
            jax.ShapeDtypeStruct((8, LIVE, MSG), BF16),
            jax.ShapeDtypeStruct((SIDE, SIDE, PIECE, WIDTH), BF16),
        ),
        in_specs=[spec(pltpu.VMEM)] * 3,
        out_specs=(spec(pltpu.VMEM),) * 2,
        scratch_shapes=[pltpu.VMEM((RESPONSES, 8 * SLOTS, MSG), BF16)] * 2,
        compiler_params=pltpu.CompilerParams(vmem_limit_bytes=VMEM_LIMIT),
    )(recv, slots, kv)
    back, grads = pl.pallas_call(
        return_kernel,
        out_shape=(
            jax.ShapeDtypeStruct((8, LIVE, MSG), BF16),
            jax.ShapeDtypeStruct((8, 2, ROWS, WIDTH), BF16),
        ),
        in_specs=[spec(pl.ANY)] * 2,
        out_specs=(spec(pl.ANY),) * 2,
        scratch_shapes=[
            pltpu.VMEM((SIDE, PIECE, WIDTH), BF16),
            pltpu.VMEM((3, SIDE, PIECE, WIDTH), BF16),
            pltpu.VMEM((SIDE, PIECE, WIDTH), BF16),
            pltpu.VMEM((3, PIECE, WIDTH), BF16),
            pltpu.VMEM((PIECE, WIDTH), F32),
            DMA, DMA((8,)), DMA((8,)), DMA((4, 3)), DMA((4, 3)), DMA((3,)), DMA((3,)), DMA((8, 2)), DMA((8, 2)), DMA((3,)),
        ],
        compiler_params=pltpu.CompilerParams(collective_id=1, has_side_effects=True, vmem_limit_bytes=VMEM_LIMIT),
    )(ret, dkv)
    wide = pl.BlockSpec((TOKENS, GW), lambda h, *_: (0, h))
    narrow = pl.BlockSpec((TOKENS, WIDTH), lambda h, *_: (0, h))
    prefix = pl.BlockSpec((ROWS, WIDTH), lambda h, *_: (0, h))
    outs = pl.pallas_call(
        unpack_kernel,
        grid_spec=pltpu.PrefetchScalarGridSpec(
            num_scalar_prefetch=2,
            grid=(KEY_HEADS,),
            in_specs=[
                pl.BlockSpec((1, LIVE, MSG), lambda h, *_: (h, 0, 0)),
                pl.BlockSpec((1, 2, ROWS, WIDTH), lambda h, *_: (h, 0, 0, 0)),
            ],
            out_specs=[wide, wide, narrow, narrow, prefix, prefix],
            scratch_shapes=[pltpu.VMEM((LIVE, TOKENS), BF16)],
        ),
        out_shape=[
            jax.ShapeDtypeStruct(q.shape, BF16),
            jax.ShapeDtypeStruct(q.shape, BF16),
            jax.ShapeDtypeStruct(k.shape, BF16),
            jax.ShapeDtypeStruct(k.shape, BF16),
            jax.ShapeDtypeStruct(pk.shape, F32),
            jax.ShapeDtypeStruct(pk.shape, F32),
        ],
        compiler_params=pltpu.CompilerParams(vmem_limit_bytes=VMEM_LIMIT),
    )(lens, prompts, back, grads)
    shapes = (queries, queries, response_keys, response_keys, prompt_prefix_keys, prompt_prefix_keys)
    return tuple(out.reshape(like.shape) for out, like in zip(outs, shapes))


def solution(mesh):
    five, three = P("prompt", "resp", None, None, None), P("prompt", "resp", None)
    return jax.shard_map(
        local,
        mesh=mesh,
        in_specs=(five, five, five, five, three, three, three, three),
        out_specs=(five, five, five, five, three, three),
        check_vma=False,
    )
```

```python
import jax
import jax.numpy as jnp
from jax import lax
from jax.experimental import pallas as pl
from jax.experimental.pallas import tpu as pltpu
from jax.sharding import PartitionSpec as P

KEY_HEADS = 8
WIDTH = 128
GROUP = 5
SLOTS = 16
RESPONSES = 16
TOKENS = SLOTS * RESPONSES
LIVE = 160
PREFIX = 384
SIDE = 4
ROWS = PREFIX // 8
PIECE = 2 * PREFIX
GW = GROUP * WIDTH
MSG = 2 * GW + 2 * WIDTH
MESH = pl.DeviceIdType.MESH
BF16 = jnp.bfloat16
F32 = jnp.float32
SCALE = WIDTH**-0.5
EXP2_SCALE = SCALE * 1.4426950408889634
VMEM_LIMIT = 58 * 1024 * 1024


class Place:
    def __init__(self):
        prompt, resp = lax.axis_index("prompt"), lax.axis_index("resp")
        self.y, self.z = prompt // SIDE, prompt % SIDE
        self.x, self.c = resp // 2, resp % 2
        self.prompt, self.resp = prompt, resp
        x, y, z, c = self.x, self.y, self.z, self.c
        self.sibling = (prompt, x * 2 + 1 - c)
        self.home_slot = 2 * (x * (1 - c) + y * c) + c
        self.head = x * (1 - c) + (SIDE + y) * c
        self.line = y * (1 - c) + x * c
        self.routes = []
        for k in (2, 1, 3):
            xd, yd = (x + k) % SIDE, (y + k) % SIDE
            self.routes.append((xd, 2 * x + c, (prompt, 2 * xd)))
            self.routes.append((SIDE + yd, 2 * y + c, (yd * SIDE + z, 2 * x + 1)))
        self.routes.append(((SIDE + y) * (1 - c) + x * c, 2 * y * (1 - c) + (2 * x + 1) * c, self.sibling))
        self.routes.append((self.head, self.home_slot, None))

    def source(self, k, core):
        along = (self.x * (1 - self.c) + self.y * self.c + k) % SIDE
        prompt = self.prompt * (1 - self.c) + (along * SIDE + self.z) * self.c
        resp = (along * 2 + core) * (1 - self.c) + (2 * self.x + core) * self.c
        return 2 * along + core, (prompt, resp)

    def line_peer(self, k):
        prompt = ((self.y + k * (1 - self.c)) % SIDE) * SIDE + self.z
        return (prompt, ((self.x + k * self.c) % SIDE) * 2 + self.c)

    def z_peer(self, k):
        return (self.y * SIDE + (self.z + k) % SIDE, self.resp)

    def barrier(self):
        sem = pltpu.get_barrier_semaphore()
        peers = [self.sibling]
        for k in (1, 2, 3):
            peers.append(self.z_peer(k))
            for core in (0, 1):
                peers.append((self.prompt, ((self.x + k) % SIDE) * 2 + core))
                peers.append((((self.y + k) % SIDE) * SIDE + self.z, 2 * self.x + core))
        for peer in peers:
            pl.semaphore_signal(sem, inc=1, device_id=peer, device_id_type=MESH)
        pl.semaphore_wait(sem, len(peers))


def remote(src, dst, send, recv, device):
    return pltpu.make_async_remote_copy(
        src_ref=src, dst_ref=dst, send_sem=send, recv_sem=recv, device_id=device, device_id_type=MESH
    )


def pack_rows(len_ref, prm_ref):
    lane = lax.broadcasted_iota(jnp.int32, (1, TOKENS), 1)
    response, token = lane >> 4, lane & (SLOTS - 1)
    row = jnp.full((1, TOKENS), -1, jnp.int32)
    slot = jnp.zeros((1, TOKENS), jnp.int32)
    start = jnp.int32(0)
    for j in range(RESPONSES):
        length = len_ref[j]
        mine = response == j
        row = jnp.where(mine & (token < length), start + token, row)
        slot = jnp.where(mine, prm_ref[j] * SLOTS + token, slot)
        start = start + length
    return row, slot


def one_hot_pack(row):
    packed = lax.broadcasted_iota(jnp.int32, (LIVE, TOKENS), 0)
    return jnp.where(packed == row, 1.0, 0.0).astype(BF16)


def dot(a, b, dims):
    return lax.dot_general(a, b, (dims, ((), ())), preferred_element_type=F32)


NN = ((1,), (0,))
NT = ((1,), (1,))
TN = ((0,), (0,))


def main_kernel(
    len_ref, prm_ref, q, g, k, v, pk, pv, back, grads,
    xb, send, slot_send, recv, slots, kv, xu, ou, dkv, half_sum, got_m, got_p, line_sum, got_b, final,
    in_sem, x_send, x_recv, sl_send, sl_recv, a_send, a_recv, b_send, b_recv,
    cp_send, cp_recv, cm_send, cm_recv, f_send, f_recv,
    h_send, h_recv, gm_send, gm_recv, gp_send, gp_recv, d_send, d_recv, e_send, e_recv, r_send, r_recv, own_sem,
):
    me = Place()
    routes = me.routes
    after, before = me.z_peer(1), me.z_peer(SIDE - 1)
    plane_of = lambda k: (me.z + k) % SIDE
    piece_of = lambda offset: (me.line + offset) % SIDE

    def await_recv(ref, sem):
        remote(ref, ref, x_send.at[0], sem, me.sibling).wait_recv()

    def await_send(ref, sem):
        remote(ref, ref, sem, x_recv.at[0], me.sibling).wait_send()

    for n, (head, _, _) in enumerate(routes):
        wide = pl.ds(pl.multiple_of(head * GW, WIDTH), GW)
        narrow = pl.ds(pl.multiple_of(head * WIDTH, WIDTH), WIDTH)
        for src, cols, low, size in ((q, wide, 0, GW), (g, wide, GW, GW), (k, narrow, 2 * GW, WIDTH), (v, narrow, 2 * GW + WIDTH, WIDTH)):
            pltpu.make_async_copy(src.at[:, cols], xb.at[n, :, pl.ds(low, size)], in_sem.at[n]).start()
    me.barrier()

    for n, (head, there, device) in enumerate(routes):
        narrow = pl.ds(pl.multiple_of(head * WIDTH, WIDTH), WIDTH)
        on_y = head // SIDE
        for i, src in enumerate((pk, pv)):
            piece = me.y * (1 - on_y) + me.x * on_y
            low = (i * PREFIX + me.resp * ROWS) * (1 - on_y) + ((me.y * 2 + i) * 2 * ROWS + me.c * ROWS) * on_y
            dst = kv.at[me.z, piece, pl.ds(pl.multiple_of(low, 16), ROWS)]
            if device is None:
                pltpu.make_async_copy(src.at[:, narrow], dst, own_sem.at[1 + i]).start()
            else:
                remote(src.at[:, narrow], dst, a_send.at[n, i], a_recv.at[there, i], device).start()

    row, slot = pack_rows(len_ref, prm_ref)
    pack = one_hot_pack(row)
    slot8 = jnp.broadcast_to(slot, (8, TOKENS)).astype(F32).astype(BF16)
    slot_send[...] = dot(slot8, pack, NT)
    for n, (_, there, device) in enumerate(routes):
        if device is None:
            pltpu.make_async_copy(slot_send, slots.at[there], own_sem.at[3]).start()
        else:
            remote(slot_send, slots.at[there], sl_send.at[n], sl_recv.at[there], device).start()

    def pack_and_send(n):
        _, there, device = routes[n]
        pltpu.make_async_copy(xb.at[n], xb.at[n], in_sem.at[n]).wait()
        rows = dot(pack, xb[n], NN).astype(BF16)
        if device is None:
            recv[there] = rows
        else:
            send[n] = rows
            remote(send.at[n], recv.at[there], x_send.at[n], x_recv.at[there], device).start()

    def spread(offset):
        ref = kv.at[me.z, piece_of(offset)]
        remote(ref, ref, cp_send.at[offset], cp_recv.at[offset], after).start()
        remote(ref, ref, cm_send.at[offset], cm_recv.at[offset], before).start()

    def line_rows(k, core, i):
        sx = (me.x + k) % SIDE * (1 - me.c) + me.x * me.c
        sy = me.y * (1 - me.c) + (me.y + k) % SIDE * me.c
        low = (i * PREFIX + (2 * sx + core) * ROWS) * (1 - me.c) + ((sy * 2 + i) * 2 * ROWS + core * ROWS) * me.c
        return pl.ds(pl.multiple_of(low, 16), ROWS)

    pack_and_send(0)
    pack_and_send(1)
    for i in (0, 1):
        dst = kv.at[me.z, me.line, line_rows(0, 0, i)]
        pltpu.make_async_copy(dst, dst, own_sem.at[1 + i]).wait()
    for k in range(SIDE):
        for core in (0, 1):
            there, _ = me.source(k, core)
            for i in (0, 1):
                dst = kv.at[me.z, me.line, line_rows(k, core, i)]
                if k == 0:
                    pl.when(me.c != core)(lambda dst=dst, there=there, i=i: await_recv(dst, a_recv.at[there, i]))
                else:
                    await_recv(dst, a_recv.at[there, i])
    for k in (1, 3, 2):
        ref = kv.at[me.z, me.line]
        remote(ref, ref, b_send.at[k - 1], b_recv.at[k - 1], me.line_peer(k)).start()
    spread(0)
    pack_and_send(2)
    pack_and_send(3)
    for k in (1, 3, 2):
        await_recv(kv.at[me.z, piece_of(k)], b_recv.at[SIDE - k - 1])
        spread(k)
    for n in range(4, 8):
        pack_and_send(n)
    for offset in (0, 1):
        ref = kv.at[plane_of(3), piece_of(offset)]
        await_recv(ref, cp_recv.at[offset])
        remote(ref, ref, f_send.at[offset], f_recv.at[offset], after).start()
    for offset in (3, 2):
        ref = kv.at[plane_of(1), piece_of(offset)]
        await_recv(ref, cm_recv.at[offset])
        remote(ref, ref, f_send.at[offset], f_recv.at[offset], before).start()

    def one_hot(i):
        slot = slots[i][0:1].astype(jnp.int32)
        return jnp.where(lax.broadcasted_iota(jnp.int32, (TOKENS, LIVE), 0) == slot, 1.0, 0.0).astype(BF16)

    pltpu.make_async_copy(slot_send, slots.at[me.home_slot], own_sem.at[3]).wait()

    def unpack(m, carry):
        there = (me.home_slot + m) % 8

        @pl.when(m > 0)
        def _():
            await_recv(slots.at[there], sl_recv.at[there])
            await_recv(recv.at[there], x_recv.at[there])

        rows = dot(one_hot(there), recv[there], NN).astype(BF16)
        xu[:, pl.ds(pl.multiple_of(there * SLOTS, SLOTS), SLOTS), :] = rows.reshape(RESPONSES, SLOTS, MSG)
        return carry

    lax.fori_loop(0, 8, unpack, 0)
    for offset in (0, 1):
        await_recv(kv.at[plane_of(1), piece_of(offset)], cm_recv.at[offset])
    for offset in (3, 2):
        await_recv(kv.at[plane_of(3), piece_of(offset)], cp_recv.at[offset])
    for offset in (0, 1, 3, 2):
        await_recv(kv.at[plane_of(2), piece_of(offset)], f_recv.at[offset])

    own_rows = lax.broadcasted_iota(jnp.int32, (WIDTH, WIDTH), 0)
    own_cols = lax.broadcasted_iota(jnp.int32, (WIDTH, WIDTH), 1)
    own_mask = (own_rows >> 4 == own_cols >> 4) & (own_cols <= own_rows)
    own_mask = jnp.concatenate([own_mask] * GROUP, axis=0)
    c = me.c

    def prompt(gz, gy):
        number = gy * SIDE + gz

        def chunk(i, quarter):
            piece = gy * (1 - c) + quarter * c
            low = (i * PREFIX + quarter * 96) * (1 - c) + (gy * 2 + i) * 96 * c
            return gz, piece, pl.ds(pl.multiple_of(low, 16), 96)

        def heads(low):
            return jnp.concatenate([xu[number, :, low + a * WIDTH : low + (a + 1) * WIDTH] for a in range(GROUP)], axis=0)

        def put(low, rows):
            ou[:, gz, pl.ds(pl.multiple_of(gy * SLOTS, SLOTS), SLOTS), low : low + WIDTH] = rows.reshape(8, SLOTS, WIDTH)

        queries, grad_rows = heads(0), heads(GW)
        keys = jnp.concatenate([kv[chunk(0, i)] for i in range(SIDE)] + [xu[number, :, 2 * GW : 2 * GW + WIDTH]], axis=0)
        values = jnp.concatenate([kv[chunk(1, i)] for i in range(SIDE)] + [xu[number, :, 2 * GW + WIDTH :]], axis=0)
        scores = dot(queries, keys, NT)
        scores = jnp.concatenate([scores[:, :PREFIX], jnp.where(own_mask, scores[:, PREFIX:], -1e30)], axis=1)
        top = jnp.max(scores, axis=1, keepdims=True)
        weights = jnp.exp2((scores - top) * EXP2_SCALE)
        over = 1.0 / jnp.sum(weights, axis=1, keepdims=True)
        half = weights.astype(BF16)
        out = dot(half, values, NN) * over
        scaled = (grad_rows.astype(F32) * over).astype(BF16)
        row_dot = jnp.sum(scaled.astype(F32) * out, axis=1, keepdims=True)
        score_grad = (weights * (dot(scaled, values, NT) - row_dot)).astype(BF16)
        query_grad = dot(score_grad, keys, NN) * SCALE
        key_grad = (dot(score_grad, queries, TN) * SCALE).astype(BF16)
        value_grad = dot(half, scaled, TN).astype(BF16)
        for i, rows in enumerate((key_grad, value_grad)):
            for quarter in range(SIDE):
                dkv[chunk(i, quarter)] = rows[quarter * 96 : (quarter + 1) * 96]
        for a in range(GROUP):
            put(a * WIDTH, out[a * WIDTH : (a + 1) * WIDTH].astype(BF16))
            put(GW + a * WIDTH, query_grad[a * WIDTH : (a + 1) * WIDTH].astype(BF16))
        put(2 * GW, key_grad[PREFIX:])
        put(2 * GW + WIDTH, value_grad[PREFIX:])

    def to_after(offset):
        remote(dkv.at[plane_of(1), piece_of(offset)], got_m.at[offset], gm_send.at[offset], gm_recv.at[offset], after).start()

    def to_before(offset):
        remote(dkv.at[plane_of(3), piece_of(offset)], got_p.at[offset], gp_send.at[offset], gp_recv.at[offset], before).start()

    def plane(s, carry):
        gz = (me.z + 6 - s - s // 2 + 2 * (s // 3)) % SIDE

        def step(gy, inner):
            prompt(gz, gy)
            return inner

        lax.fori_loop(0, SIDE, step, 0)

        @pl.when(s == 0)
        def _():
            for offset in range(SIDE):
                device = after if offset < 2 else before
                remote(dkv.at[plane_of(2), piece_of(offset)], half_sum.at[offset], h_send.at[offset], h_recv.at[offset], device).start()

        @pl.when(s == 1)
        def _():
            to_after(2)
            to_after(3)

        @pl.when(s == 2)
        def _():
            to_before(0)
            to_before(1)
            for offset in range(SIDE):
                there = plane_of(1) if offset < 2 else plane_of(3)
                await_recv(half_sum.at[offset], h_recv.at[offset])
                total = dkv[there, piece_of(offset)].astype(F32) + half_sum[offset].astype(F32)
                dkv[there, piece_of(offset)] = total.astype(BF16)
                if offset < 2:
                    to_after(offset)
                else:
                    to_before(offset)

        for k in (2, 1, 3, 0):
            for core in (0, 1):
                there, device = me.source(k, core)
                index = 2 * k + core
                src, dst = ou.at[there, gz], back.at[me.head, gz]
                away = lambda: remote(src, dst, r_send.at[index], r_recv.at[me.head], device).start()
                if k == 0:
                    pl.when(c == core)(lambda: pltpu.make_async_copy(src, dst, own_sem.at[0]).start())
                    pl.when(c != core)(away)
                else:
                    away()
        return carry

    lax.fori_loop(0, SIDE, plane, 0)

    for offset in (1, 3, 2, 0):
        await_recv(got_m.at[offset], gm_recv.at[offset])
        await_recv(got_p.at[offset], gp_recv.at[offset])
        total = dkv[me.z, piece_of(offset)].astype(F32) + got_m[offset].astype(F32) + got_p[offset].astype(F32)
        if offset == 0:
            final[...] = total
        else:
            line_sum[offset - 1] = total.astype(BF16)
            remote(line_sum.at[offset - 1], got_b.at[offset - 1], d_send.at[offset - 1], d_recv.at[offset - 1], me.line_peer(offset)).start()
    for k in (1, 3, 2):
        await_recv(got_b.at[k - 1], d_recv.at[k - 1])
    line_sum[3] = (final[...] + got_b[0].astype(F32) + got_b[1].astype(F32) + got_b[2].astype(F32)).astype(BF16)
    for k in (2, 1, 3, 0):
        for core in (0, 1):
            _, device = me.source(k, core)
            index = 2 * k + core
            for i in (0, 1):
                src, dst = line_sum.at[3, line_rows(k, core, i)], grads.at[me.head, i]
                away = lambda: remote(src, dst, e_send.at[index, i], e_recv.at[me.head, i], device).start()
                if k == 0:
                    pl.when(c == core)(lambda: pltpu.make_async_copy(src, dst, own_sem.at[1 + i]).start())
                    pl.when(c != core)(away)
                else:
                    away()

    for head, _, device in routes:
        if device is None:
            pltpu.make_async_copy(back.at[head], back.at[head], own_sem.at[0]).wait()
            for i in (0, 1):
                pltpu.make_async_copy(grads.at[head, i], grads.at[head, i], own_sem.at[1 + i]).wait()
        else:
            await_recv(back.at[head], r_recv.at[head])
            for i in (0, 1):
                await_recv(grads.at[head, i], e_recv.at[head, i])
    for n in range(7):
        await_send(send.at[n], x_send.at[n])
        await_send(slot_send, sl_send.at[n])
        for i in (0, 1):
            await_send(grads.at[0, i], a_send.at[n, i])
    for k in range(3):
        await_send(line_sum.at[k], b_send.at[k])
        await_send(line_sum.at[k], d_send.at[k])
    for offset in range(SIDE):
        for sem in (cp_send, cm_send, f_send, h_send, gm_send, gp_send):
            await_send(got_m.at[offset], sem.at[offset])

    def sent_back(index):
        await_send(back.at[0], r_send.at[index])
        for i in (0, 1):
            await_send(grads.at[0, i], e_send.at[index, i])

    for index in range(8):
        if index < 2:
            pl.when(c != index)(lambda: sent_back(index))
        else:
            sent_back(index)


def unpack_kernel(len_ref, prm_ref, back, grads, attn, query, key, value, prefix_key, prefix_value, pick):
    @pl.when(pl.program_id(0) == 0)
    def _():
        lane = lax.broadcasted_iota(jnp.int32, (SLOTS, TOKENS), 1)
        token = lax.broadcasted_iota(jnp.int32, (SLOTS, TOKENS), 0)
        for j in range(RESPONSES):
            there = prm_ref[j]
            first = (there % SIDE) * SIDE * SLOTS + (there // SIDE) * SLOTS
            mine = (lane == first + token) & (token < len_ref[j])
            pick[j * SLOTS : (j + 1) * SLOTS, :] = jnp.where(mine, 1.0, 0.0).astype(BF16)

    rows = dot(pick[...], back[0].reshape(TOKENS, MSG), NN).astype(BF16)
    attn[...] = rows[:, :GW]
    query[...] = rows[:, GW : 2 * GW]
    key[...] = rows[:, 2 * GW : 2 * GW + WIDTH]
    value[...] = rows[:, 2 * GW + WIDTH :]
    prefix_key[...] = grads[0, 0].astype(F32)
    prefix_value[...] = grads[0, 1].astype(F32)


def spec(space):
    return pl.BlockSpec(memory_space=space)


DMA = pltpu.SemaphoreType.DMA


def local(queries, grad_out, response_keys, response_values, prompt_prefix_keys, prompt_prefix_values, lengths, prompt_of):
    q, g = queries.reshape(TOKENS, KEY_HEADS * GW), grad_out.reshape(TOKENS, KEY_HEADS * GW)
    k, v = response_keys.reshape(TOKENS, KEY_HEADS * WIDTH), response_values.reshape(TOKENS, KEY_HEADS * WIDTH)
    pk, pv = prompt_prefix_keys.reshape(ROWS, KEY_HEADS * WIDTH), prompt_prefix_values.reshape(ROWS, KEY_HEADS * WIDTH)
    lens, prompts = lengths.reshape(RESPONSES), prompt_of.reshape(RESPONSES)
    vmem = pltpu.VMEM
    back, grads = pl.pallas_call(
        main_kernel,
        out_shape=(
            jax.ShapeDtypeStruct((8, SIDE, SIDE * SLOTS, MSG), BF16),
            jax.ShapeDtypeStruct((8, 2, ROWS, WIDTH), BF16),
        ),
        in_specs=[spec(pltpu.SMEM)] * 2 + [spec(pl.ANY)] * 6,
        out_specs=(spec(pl.ANY),) * 2,
        scratch_shapes=[
            vmem((8, TOKENS, MSG), BF16), vmem((7, LIVE, MSG), BF16), vmem((8, LIVE), F32),
            vmem((8, LIVE, MSG), BF16), vmem((8, 8, LIVE), F32), vmem((SIDE, SIDE, PIECE, WIDTH), BF16),
            vmem((RESPONSES, 8 * SLOTS, MSG), BF16), vmem((8, SIDE, SIDE * SLOTS, MSG), BF16),
            vmem((SIDE, SIDE, PIECE, WIDTH), BF16), vmem((SIDE, PIECE, WIDTH), BF16), vmem((SIDE, PIECE, WIDTH), BF16),
            vmem((SIDE, PIECE, WIDTH), BF16), vmem((SIDE, PIECE, WIDTH), BF16), vmem((3, PIECE, WIDTH), BF16), vmem((PIECE, WIDTH), F32),
            DMA((8,)), DMA((8,)), DMA((8,)), DMA((8,)), DMA((8,)), DMA((8, 2)), DMA((8, 2)), DMA((3,)), DMA((3,)),
        ] + [DMA((SIDE,))] * 12 + [DMA((3,)), DMA((3,)), DMA((8, 2)), DMA((8, 2)), DMA((8,)), DMA((8,)), DMA((4,))],
        compiler_params=pltpu.CompilerParams(collective_id=0, has_side_effects=True, vmem_limit_bytes=VMEM_LIMIT),
    )(lens, prompts, q, g, k, v, pk, pv)
    wide = pl.BlockSpec((TOKENS, GW), lambda h, *_: (0, h))
    narrow = pl.BlockSpec((TOKENS, WIDTH), lambda h, *_: (0, h))
    prefix = pl.BlockSpec((ROWS, WIDTH), lambda h, *_: (0, h))
    outs = pl.pallas_call(
        unpack_kernel,
        grid_spec=pltpu.PrefetchScalarGridSpec(
            num_scalar_prefetch=2,
            grid=(KEY_HEADS,),
            in_specs=[
                pl.BlockSpec((1, SIDE, SIDE * SLOTS, MSG), lambda h, *_: (h, 0, 0, 0)),
                pl.BlockSpec((1, 2, ROWS, WIDTH), lambda h, *_: (h, 0, 0, 0)),
            ],
            out_specs=[wide, wide, narrow, narrow, prefix, prefix],
            scratch_shapes=[vmem((TOKENS, TOKENS), BF16)],
        ),
        out_shape=[
            jax.ShapeDtypeStruct(q.shape, BF16),
            jax.ShapeDtypeStruct(q.shape, BF16),
            jax.ShapeDtypeStruct(k.shape, BF16),
            jax.ShapeDtypeStruct(k.shape, BF16),
            jax.ShapeDtypeStruct(pk.shape, F32),
            jax.ShapeDtypeStruct(pk.shape, F32),
        ],
        compiler_params=pltpu.CompilerParams(vmem_limit_bytes=VMEM_LIMIT),
    )(lens, prompts, back, grads)
    shapes = (queries, queries, response_keys, response_keys, prompt_prefix_keys, prompt_prefix_keys)
    return tuple(out.reshape(like.shape) for out, like in zip(outs, shapes))


def solution(mesh):
    five, three = P("prompt", "resp", None, None, None), P("prompt", "resp", None)
    return jax.shard_map(
        local,
        mesh=mesh,
        in_specs=(five, five, five, five, three, three, three, three),
        out_specs=(five, five, five, five, three, three),
        check_vma=False,
    )
```

```python
import jax
import jax.numpy as jnp
from jax import lax
from jax.experimental import pallas as pl
from jax.experimental.pallas import tpu as pltpu
from jax.sharding import PartitionSpec as P

KEY_HEADS = 8
WIDTH = 128
GROUP = 5
SLOTS = 16
RESPONSES = 16
TOKENS = SLOTS * RESPONSES
LIVE = 160
PREFIX = 384
SIDE = 4
ROWS = PREFIX // 8
GW = GROUP * WIDTH
MSG = 2 * GW + 2 * WIDTH
MESH = pl.DeviceIdType.MESH
BF16 = jnp.bfloat16
F32 = jnp.float32
SCALE = WIDTH**-0.5
EXP2_SCALE = SCALE * 1.4426950408889634
BATCH = 4
HOLD = 14
EARLY = 0
SHIFT = 0
VMEM_LIMIT = 58 * 1024 * 1024


class Place:
    def __init__(self):
        prompt, resp = lax.axis_index("prompt"), lax.axis_index("resp")
        self.y, self.z = prompt // SIDE, prompt % SIDE
        self.x, self.c = resp // 2, resp % 2
        self.prompt, self.resp = prompt, resp
        x, y, z, c = self.x, self.y, self.z, self.c
        self.sibling = (prompt, x * 2 + 1 - c)
        self.home_slot = 2 * (x * (1 - c) + y * c) + c
        self.head = x * (1 - c) + (SIDE + y) * c
        self.line = y * (1 - c) + x * c
        self.routes = []
        for k in (2, 1, 3):
            xd, yd = (x + k) % SIDE, (y + k) % SIDE
            self.routes.append((xd, 2 * x + c, (prompt, 2 * xd)))
            self.routes.append((SIDE + yd, 2 * y + c, (yd * SIDE + z, 2 * x + 1)))
        self.routes.append(((SIDE + y) * (1 - c) + x * c, 2 * y * (1 - c) + (2 * x + 1) * c, self.sibling))
        self.routes.append((self.head, self.home_slot, None))

    def source(self, k, core):
        along = (self.x * (1 - self.c) + self.y * self.c + k) % SIDE
        prompt = self.prompt * (1 - self.c) + (along * SIDE + self.z) * self.c
        resp = (along * 2 + core) * (1 - self.c) + (2 * self.x + core) * self.c
        return 2 * along + core, (prompt, resp)

    def line_peer(self, k):
        prompt = ((self.y + k * (1 - self.c)) % SIDE) * SIDE + self.z
        return (prompt, ((self.x + k * self.c) % SIDE) * 2 + self.c)

    def z_peer(self, k):
        return (self.y * SIDE + (self.z + k) % SIDE, self.resp)

    def barrier(self):
        sem = pltpu.get_barrier_semaphore()
        peers = [self.sibling]
        for k in (1, 2, 3):
            peers.append(self.z_peer(k))
            for core in (0, 1):
                peers.append((self.prompt, ((self.x + k) % SIDE) * 2 + core))
                peers.append((((self.y + k) % SIDE) * SIDE + self.z, 2 * self.x + core))
        for peer in peers:
            pl.semaphore_signal(sem, inc=1, device_id=peer, device_id_type=MESH)
        pl.semaphore_wait(sem, len(peers))


def remote(src, dst, send, recv, device):
    return pltpu.make_async_remote_copy(
        src_ref=src, dst_ref=dst, send_sem=send, recv_sem=recv, device_id=device, device_id_type=MESH
    )


def pack_rows(len_ref, prm_ref):
    lane = lax.broadcasted_iota(jnp.int32, (1, TOKENS), 1)
    response, token = lane >> 4, lane & (SLOTS - 1)
    row = jnp.full((1, TOKENS), -1, jnp.int32)
    slot = jnp.zeros((1, TOKENS), jnp.int32)
    start = jnp.int32(0)
    for j in range(RESPONSES):
        length = len_ref[j]
        mine = response == j
        row = jnp.where(mine & (token < length), start + token, row)
        slot = jnp.where(mine, prm_ref[j] * SLOTS + token, slot)
        start = start + length
    return row, slot


def one_hot_pack(row):
    packed = lax.broadcasted_iota(jnp.int32, (LIVE, TOKENS), 0)
    return jnp.where(packed == row, 1.0, 0.0).astype(BF16)


def dot(a, b, dims):
    return lax.dot_general(a, b, (dims, ((), ())), preferred_element_type=F32)


NN = ((1,), (0,))
NT = ((1,), (1,))
TN = ((0,), (0,))


def main_kernel(
    len_ref, prm_ref, q, g, k, v, pk, pv, back, grads,
    xb, send, slot_send, recv, slots, kv, pkv, xu, ou, dkv, half_sum, got_m, got_p, plane_sum, got_y, got_x, final_y, final_x,
    in_sem, x_send, x_recv, sl_send, sl_recv, a_send, a_recv, b_send, b_recv,
    cp_send, cp_recv, cm_send, cm_recv, f_send, f_recv,
    h_send, h_recv, gm_send, gm_recv, gp_send, gp_recv, d_send, d_recv, e_send, e_recv, r_send, r_recv, own_sem,
):
    me = Place()
    routes = me.routes
    after, before = me.z_peer(1), me.z_peer(SIDE - 1)
    plane_of = lambda k: (me.z + k) % SIDE
    piece_of = lambda offset: (me.line + offset) % SIDE

    def core_rows(core):
        return pl.ds(pl.multiple_of(core * ROWS, 16), ROWS)

    def await_recv(ref, sem):
        remote(ref, ref, x_send.at[0], sem, me.sibling).wait_recv()

    def await_send(ref, sem):
        remote(ref, ref, sem, x_recv.at[0], me.sibling).wait_send()

    for n, (head, _, _) in enumerate(routes):
        wide = pl.ds(pl.multiple_of(head * GW, WIDTH), GW)
        narrow = pl.ds(pl.multiple_of(head * WIDTH, WIDTH), WIDTH)
        for src, cols, low, size in ((q, wide, 0, GW), (g, wide, GW, GW), (k, narrow, 2 * GW, WIDTH), (v, narrow, 2 * GW + WIDTH, WIDTH)):
            pltpu.make_async_copy(src.at[:, cols], xb.at[n, :, pl.ds(low, size)], in_sem.at[n]).start()
    for i, src in enumerate((pk, pv)):
        pltpu.make_async_copy(src, pkv.at[i], own_sem.at[2]).start()
    me.barrier()
    pltpu.make_async_copy(pkv, pkv, own_sem.at[2]).wait()

    for n, (head, there, device) in enumerate(routes):
        narrow = pl.ds(pl.multiple_of(head * WIDTH, WIDTH), WIDTH)
        on_y = head // SIDE
        piece, part = me.y * (1 - on_y) + me.x * on_y, me.x * (1 - on_y) + me.y * on_y
        src, dst = pkv.at[:, :, narrow], kv.at[me.z, piece, part, :, core_rows(me.c)]
        if device is None:
            pltpu.make_async_copy(src, dst, own_sem.at[1]).start()
        else:
            remote(src, dst, a_send.at[n], a_recv.at[there], device).start()

    row, slot = pack_rows(len_ref, prm_ref)
    pack = one_hot_pack(row)
    slot8 = jnp.broadcast_to(slot, (8, TOKENS)).astype(F32).astype(BF16)
    slot_send[...] = dot(slot8, pack, NT)
    for n, (_, there, device) in enumerate(routes):
        if device is None:
            pltpu.make_async_copy(slot_send, slots.at[there], own_sem.at[3]).start()
        else:
            remote(slot_send, slots.at[there], sl_send.at[n], sl_recv.at[there], device).start()

    def pack_rows_of(n):
        _, there, device = routes[n]
        pltpu.make_async_copy(xb.at[n], xb.at[n], in_sem.at[n]).wait()
        rows = dot(pack, xb[n], NN).astype(BF16)
        if device is None:
            recv[there] = rows
        else:
            send[n] = rows

    def send_rows(n):
        _, there, device = routes[n]
        if device is not None:
            remote(send.at[n], recv.at[there], x_send.at[n], x_recv.at[there], device).start()

    def pass_on(offset, ahead, sem, device):
        ref = kv.at[plane_of(ahead), piece_of(offset)]
        await_recv(ref, sem.at[offset])
        remote(ref, ref, f_send.at[offset], f_recv.at[offset], device).start()

    def spread(offset):
        ref = kv.at[me.z, piece_of(offset)]
        remote(ref, ref, cp_send.at[offset], cp_recv.at[offset], after).start()
        remote(ref, ref, cm_send.at[offset], cm_recv.at[offset], before).start()

    pack_rows_of(0)
    for n in range(EARLY):
        send_rows(n)
        pack_rows_of(n + 1)
    for k in range(SIDE):
        for core in (0, 1):
            there, _ = me.source(k, core)
            dst = kv.at[me.z, me.line, there // 2, :, core_rows(core)]
            if k == 0:
                pl.when(me.c == core)(lambda dst=dst: pltpu.make_async_copy(dst, dst, own_sem.at[1]).wait())
                pl.when(me.c != core)(lambda dst=dst, there=there: await_recv(dst, a_recv.at[there]))
            else:
                await_recv(dst, a_recv.at[there])
    for k in (1, 3, 2):
        ref = kv.at[me.z, me.line]
        remote(ref, ref, b_send.at[k - 1], b_recv.at[k - 1], me.line_peer(k)).start()
    spread(0)
    for n in range(EARLY, 4):
        if n > EARLY:
            pack_rows_of(n)
        send_rows(n)
    for k in (1, 3, 2):
        await_recv(kv.at[me.z, piece_of(k)], b_recv.at[SIDE - k - 1])
        spread(k)
        if k == 1:
            pass_on(0, 3, cp_recv, after)
        n = {1: 4, 3: 5, 2: 6}[k]
        pack_rows_of(n)
        send_rows(n)
    pack_rows_of(7)
    pass_on(1, 3, cp_recv, after)
    pass_on(3, 1, cm_recv, before)
    pass_on(2, 1, cm_recv, before)
    def one_hot(i):
        slot = slots[i][0:1].astype(jnp.int32)
        return jnp.where(lax.broadcasted_iota(jnp.int32, (TOKENS, LIVE), 0) == slot, 1.0, 0.0).astype(BF16)

    pltpu.make_async_copy(slot_send, slots.at[me.home_slot], own_sem.at[3]).wait()

    def unpack(m, carry):
        ahead = 2 + m // 2 + m // 4 + 2 * (m // 6)
        there = 2 * ((me.home_slot // 2 + ahead) % SIDE) + m % 2

        @pl.when(there != me.home_slot)
        def _():
            await_recv(slots.at[there], sl_recv.at[there])
            await_recv(recv.at[there], x_recv.at[there])

        rows = dot(one_hot(there), recv[there], NN).astype(BF16)
        xu[:, pl.ds(pl.multiple_of(there * SLOTS, SLOTS), SLOTS), :] = rows.reshape(RESPONSES, SLOTS, MSG)
        return carry

    lax.fori_loop(0, 8, unpack, 0)
    own_rows = lax.broadcasted_iota(jnp.int32, (WIDTH, WIDTH), 0)
    own_cols = lax.broadcasted_iota(jnp.int32, (WIDTH, WIDTH), 1)
    own_mask = (own_rows >> 4 == own_cols >> 4) & (own_cols <= own_rows)
    own_mask = jnp.concatenate([own_mask] * GROUP, axis=0)
    c = me.c

    def prompt(gz, gy):
        number = gy * SIDE + gz

        def chunk(i, quarter):
            return gz, gy * (1 - c) + quarter * c, quarter * (1 - c) + gy * c, i

        def heads(low):
            return jnp.concatenate([xu[number, :, low + a * WIDTH : low + (a + 1) * WIDTH] for a in range(GROUP)], axis=0)

        def put(low, rows):
            ou[:, gz, pl.ds(pl.multiple_of(gy * SLOTS, SLOTS), SLOTS), low : low + WIDTH] = rows.reshape(8, SLOTS, WIDTH)

        queries, grad_rows = heads(0), heads(GW)
        keys = jnp.concatenate([kv[chunk(0, i)] for i in range(SIDE)] + [xu[number, :, 2 * GW : 2 * GW + WIDTH]], axis=0)
        values = jnp.concatenate([kv[chunk(1, i)] for i in range(SIDE)] + [xu[number, :, 2 * GW + WIDTH :]], axis=0)
        scores = dot(queries, keys, NT)
        scores = jnp.concatenate([scores[:, :PREFIX], jnp.where(own_mask, scores[:, PREFIX:], -1e30)], axis=1)
        top = jnp.max(scores, axis=1, keepdims=True)
        weights = jnp.exp2((scores - top) * EXP2_SCALE)
        over = 1.0 / jnp.sum(weights, axis=1, keepdims=True)
        half = weights.astype(BF16)
        out = dot(half, values, NN) * over
        scaled = (grad_rows.astype(F32) * over).astype(BF16)
        row_dot = jnp.sum(scaled.astype(F32) * out, axis=1, keepdims=True)
        score_grad = (weights * (dot(scaled, values, NT) - row_dot)).astype(BF16)
        query_grad = dot(score_grad, keys, NN) * SCALE
        key_grad = (dot(score_grad, queries, TN) * SCALE).astype(BF16)
        value_grad = dot(half, scaled, TN).astype(BF16)
        dkv[gz, gy, 0] = key_grad[:PREFIX]
        dkv[gz, gy, 1] = value_grad[:PREFIX]
        for a in range(GROUP):
            put(a * WIDTH, out[a * WIDTH : (a + 1) * WIDTH].astype(BF16))
            put(GW + a * WIDTH, query_grad[a * WIDTH : (a + 1) * WIDTH].astype(BF16))
        put(2 * GW, key_grad[PREFIX:])
        put(2 * GW + WIDTH, value_grad[PREFIX:])

    def send_back(gz, gy):
        rows = pl.ds(pl.multiple_of(gy * SLOTS, SLOTS), SLOTS)
        for k in (2, 1, 3, 0):
            for core in (0, 1):
                there, device = me.source(k, core)
                index = 2 * k + core
                src, dst = ou.at[there, gz, rows], back.at[me.head, gz, rows]
                away = lambda: remote(src, dst, r_send.at[index], r_recv.at[me.head], device).start()
                if k == 0:
                    pl.when(c == core)(lambda: pltpu.make_async_copy(src, dst, own_sem.at[0]).start())
                    pl.when(c != core)(away)
                else:
                    away()

    def plan(n):
        quarter, odd = n // 4, n % 2
        first, middle = 1 - (quarter + 3) // 4, (quarter * (3 - quarter)) // 2
        ahead = first * 2 + middle * (1 + 2 * odd)
        gy = first * (odd * 2 + n // 2) + middle * (((n + 4) // 2 + 2 * (1 - odd)) % SIDE) + (1 - first - middle) * (n % SIDE)
        return (me.z + ahead) % SIDE, gy

    def step(count, carry):
        n = (count + SHIFT) % RESPONSES
        gz, gy = plan(n)

        @pl.when(n == 0)
        def _():
            for offset in (0, 3, 1, 2):
                await_recv(kv.at[plane_of(2), piece_of(offset)], f_recv.at[offset])

        @pl.when(n == 4)
        def _():
            for offset in (0, 1):
                await_recv(kv.at[plane_of(1), piece_of(offset)], cm_recv.at[offset])
            for offset in (3, 2):
                await_recv(kv.at[plane_of(3), piece_of(offset)], cp_recv.at[offset])

        prompt(gz, gy)

        @pl.when((n >= 8) & (n < 12))
        def _():
            await_recv(half_sum.at[gy], h_recv.at[gy])
            dkv[gz, gy] = (dkv[gz, gy].astype(F32) + half_sum[gy].astype(F32)).astype(BF16)

        for odd, device, got, send_sem, recv_sem in ((0, after, got_m, gm_send, gm_recv), (1, before, got_p, gp_send, gp_recv)):

            @pl.when((n < 4) & (n % 2 == odd))
            def _():
                remote(dkv.at[gz, gy], half_sum.at[gy], h_send.at[gy], h_recv.at[gy], device).start()

            @pl.when((n >= 4) & (n < 12) & (n % 2 == odd))
            def _():
                remote(dkv.at[gz, gy], got.at[gy], send_sem.at[gy], recv_sem.at[gy], device).start()

        @pl.when(count < HOLD)
        def _():
            send_back(gz, gy)

        return carry

    lax.fori_loop(0, RESPONSES, step, 0)

    def add_up(gy, carry):
        await_recv(got_m.at[gy], gm_recv.at[gy])
        await_recv(got_p.at[gy], gp_recv.at[gy])
        total = dkv[me.z, gy].astype(F32) + got_m[gy].astype(F32) + got_p[gy].astype(F32)
        plane_sum[gy] = total.astype(BF16)
        return carry

    lax.fori_loop(0, SIDE, add_up, 0)

    def columns(k):
        return pl.ds(pl.multiple_of((me.x + k) % SIDE * 96, 16), 96)

    @pl.when(c == 0)
    def _():
        for k in (2, 1, 3):
            remote(plane_sum.at[(me.y + k) % SIDE], got_y.at[k - 1], d_send.at[k - 1], d_recv.at[k - 1], me.line_peer(k)).start()

    @pl.when(c != 0)
    def _():
        for k in (2, 1, 3):
            remote(plane_sum.at[:, :, columns(k)], got_x.at[k - 1], d_send.at[k - 1], d_recv.at[k - 1], me.line_peer(k)).start()

    def late(n, carry):
        send_back(*plan((n + SHIFT) % RESPONSES))
        return carry

    lax.fori_loop(HOLD, RESPONSES, late, 0)

    def send_grads(part):
        for k in (2, 1, 3, 0):
            for core in (0, 1):
                _, device = me.source(k, core)
                index = 2 * k + core
                src, dst = part(k, core), grads.at[me.head]
                if k > 0 or core == 1 - part.core:
                    remote(src, dst, e_send.at[index], e_recv.at[me.head], device).start()
                else:
                    pltpu.make_async_copy(src, dst, own_sem.at[1]).start()

    @pl.when(c == 0)
    def _():
        total = plane_sum[me.y].astype(F32)
        for k in (1, 3, 2):
            await_recv(got_y.at[k - 1], d_recv.at[k - 1])
            total = total + got_y[k - 1].astype(F32)
        final_y[...] = total.astype(BF16)

        def part(k, core):
            return final_y.at[:, pl.ds(pl.multiple_of((2 * ((me.x + k) % SIDE) + core) * ROWS, 16), ROWS)]

        part.core = 0
        send_grads(part)

    @pl.when(c != 0)
    def _():
        total = plane_sum[:, :, columns(0)].astype(F32)
        for k in (1, 3, 2):
            await_recv(got_x.at[k - 1], d_recv.at[k - 1])
            total = total + got_x[k - 1].astype(F32)
        final_x[...] = total.astype(BF16)

        def part(k, core):
            return final_x.at[(me.y + k) % SIDE, :, pl.ds(core * ROWS, ROWS)]

        part.core = 1
        send_grads(part)

    for head, _, device in routes:
        if device is None:
            pltpu.make_async_copy(back.at[head], back.at[head], own_sem.at[0]).wait()
            pltpu.make_async_copy(grads.at[head], grads.at[head], own_sem.at[1]).wait()
        else:
            await_recv(back.at[head], r_recv.at[head])
            await_recv(grads.at[head], e_recv.at[head])
    for n in range(7):
        await_send(send.at[n], x_send.at[n])
        await_send(slot_send, sl_send.at[n])
        await_send(grads.at[0], a_send.at[n])
    for k in range(3):
        await_send(got_y.at[k], b_send.at[k])
        await_send(got_y.at[k], d_send.at[k])
    for offset in range(SIDE):
        for sem in (cp_send, cm_send, f_send, h_send, gm_send, gp_send):
            await_send(got_m.at[offset], sem.at[offset])

    def sent_back(index):
        await_send(back.at[0], r_send.at[index])
        await_send(grads.at[0], e_send.at[index])

    for index in range(8):
        if index < 2:
            pl.when(c != index)(lambda: sent_back(index))
        else:
            sent_back(index)


def place_kernel(len_ref, prm_ref, *refs):
    blocks, (grads, attn, query, key, value, prefix_key, prefix_value) = refs[:BATCH], refs[BATCH:]
    step = pl.program_id(0)
    token = lax.broadcasted_iota(jnp.int32, (SLOTS, GW), 0)
    for m, block in enumerate(blocks):
        live = token < len_ref[step * BATCH + m]
        rows = slice(m * SLOTS, (m + 1) * SLOTS)
        for h in range(KEY_HEADS):
            attn[rows, h * GW : (h + 1) * GW] = jnp.where(live, block[h, 0, :, :GW], jnp.zeros((), BF16))
            query[rows, h * GW : (h + 1) * GW] = block[h, 0, :, GW : 2 * GW]
            key[rows, h * WIDTH : (h + 1) * WIDTH] = block[h, 0, :, 2 * GW : 2 * GW + WIDTH]
            value[rows, h * WIDTH : (h + 1) * WIDTH] = block[h, 0, :, 2 * GW + WIDTH :]

    @pl.when(step == 0)
    def _():
        for h in range(KEY_HEADS):
            prefix_key[:, h * WIDTH : (h + 1) * WIDTH] = grads[h, 0].astype(F32)
            prefix_value[:, h * WIDTH : (h + 1) * WIDTH] = grads[h, 1].astype(F32)


def spec(space):
    return pl.BlockSpec(memory_space=space)


DMA = pltpu.SemaphoreType.DMA


def local(queries, grad_out, response_keys, response_values, prompt_prefix_keys, prompt_prefix_values, lengths, prompt_of):
    q, g = queries.reshape(TOKENS, KEY_HEADS * GW), grad_out.reshape(TOKENS, KEY_HEADS * GW)
    k, v = response_keys.reshape(TOKENS, KEY_HEADS * WIDTH), response_values.reshape(TOKENS, KEY_HEADS * WIDTH)
    pk, pv = prompt_prefix_keys.reshape(ROWS, KEY_HEADS * WIDTH), prompt_prefix_values.reshape(ROWS, KEY_HEADS * WIDTH)
    lens, prompts = lengths.reshape(RESPONSES), prompt_of.reshape(RESPONSES)
    vmem = pltpu.VMEM
    back, grads = pl.pallas_call(
        main_kernel,
        out_shape=(
            jax.ShapeDtypeStruct((8, SIDE, SIDE * SLOTS, MSG), BF16),
            jax.ShapeDtypeStruct((8, 2, ROWS, WIDTH), BF16),
        ),
        in_specs=[spec(pltpu.SMEM)] * 2 + [spec(pl.ANY)] * 6,
        out_specs=(spec(pl.ANY),) * 2,
        scratch_shapes=[
            vmem((8, TOKENS, MSG), BF16), vmem((7, LIVE, MSG), BF16), vmem((8, LIVE), F32),
            vmem((8, LIVE, MSG), BF16), vmem((8, 8, LIVE), F32), vmem((SIDE, SIDE, SIDE, 2, 96, WIDTH), BF16),
            vmem((2, ROWS, KEY_HEADS * WIDTH), BF16),
            vmem((RESPONSES, 8 * SLOTS, MSG), BF16), vmem((8, SIDE, SIDE * SLOTS, MSG), BF16),
            vmem((SIDE, SIDE, 2, PREFIX, WIDTH), BF16), vmem((SIDE, 2, PREFIX, WIDTH), BF16), vmem((SIDE, 2, PREFIX, WIDTH), BF16),
            vmem((SIDE, 2, PREFIX, WIDTH), BF16), vmem((SIDE, 2, PREFIX, WIDTH), BF16),
            vmem((3, 2, PREFIX, WIDTH), BF16), vmem((3, SIDE, 2, 96, WIDTH), BF16),
            vmem((2, PREFIX, WIDTH), BF16), vmem((SIDE, 2, 96, WIDTH), BF16),
            DMA((8,)), DMA((8,)), DMA((8,)), DMA((8,)), DMA((8,)), DMA((8,)), DMA((8,)), DMA((3,)), DMA((3,)),
        ] + [DMA((SIDE,))] * 12 + [DMA((3,)), DMA((3,)), DMA((8,)), DMA((8,)), DMA((8,)), DMA((8,)), DMA((4,))],
        compiler_params=pltpu.CompilerParams(collective_id=0, has_side_effects=True, vmem_limit_bytes=VMEM_LIMIT),
    )(lens, prompts, q, g, k, v, pk, pv)
    def block_of(m):
        def index(i, lens, prompts):
            there = prompts[i * BATCH + m]
            return 0, there % SIDE, there // SIDE, 0

        return pl.BlockSpec((KEY_HEADS, 1, SLOTS, MSG), index)

    wide = pl.BlockSpec((BATCH * SLOTS, KEY_HEADS * GW), lambda i, *_: (i, 0))
    narrow = pl.BlockSpec((BATCH * SLOTS, KEY_HEADS * WIDTH), lambda i, *_: (i, 0))
    prefix = pl.BlockSpec((ROWS, KEY_HEADS * WIDTH), lambda i, *_: (0, 0))
    outs = pl.pallas_call(
        place_kernel,
        grid_spec=pltpu.PrefetchScalarGridSpec(
            num_scalar_prefetch=2,
            grid=(RESPONSES // BATCH,),
            in_specs=[block_of(m) for m in range(BATCH)] + [pl.BlockSpec(grads.shape, lambda i, *_: (0, 0, 0, 0))],
            out_specs=[wide, wide, narrow, narrow, prefix, prefix],
        ),
        out_shape=[
            jax.ShapeDtypeStruct(q.shape, BF16),
            jax.ShapeDtypeStruct(q.shape, BF16),
            jax.ShapeDtypeStruct(k.shape, BF16),
            jax.ShapeDtypeStruct(k.shape, BF16),
            jax.ShapeDtypeStruct(pk.shape, F32),
            jax.ShapeDtypeStruct(pk.shape, F32),
        ],
        compiler_params=pltpu.CompilerParams(vmem_limit_bytes=VMEM_LIMIT),
    )(lens, prompts, *[back] * BATCH, grads)
    shapes = (queries, queries, response_keys, response_keys, prompt_prefix_keys, prompt_prefix_keys)
    return tuple(out.reshape(like.shape) for out, like in zip(outs, shapes))


def solution(mesh):
    five, three = P("prompt", "resp", None, None, None), P("prompt", "resp", None)
    return jax.shard_map(
        local,
        mesh=mesh,
        in_specs=(five, five, five, five, three, three, three, three),
        out_specs=(five, five, five, five, three, three),
        check_vma=False,
    )
```

```python
import jax
import jax.numpy as jnp
from jax import lax
from jax.experimental import pallas as pl
from jax.experimental.pallas import tpu as pltpu
from jax.sharding import PartitionSpec as P

KEY_HEADS = 8
WIDTH = 128
GROUP = 5
SLOTS = 16
RESPONSES = 16
TOKENS = SLOTS * RESPONSES
LIVE = 160
PREFIX = 384
SIDE = 4
ROWS = PREFIX // 8
GW = GROUP * WIDTH
MSG = 2 * GW + 2 * WIDTH
MESH = pl.DeviceIdType.MESH
BF16 = jnp.bfloat16
F32 = jnp.float32
SCALE = WIDTH**-0.5
EXP2_SCALE = SCALE * 1.4426950408889634
BATCH = 8
HOLD = 14
FIRST = 2
SHIFT = 0
VMEM_LIMIT = 58 * 1024 * 1024


class Place:
    def __init__(self):
        prompt, resp = lax.axis_index("prompt"), lax.axis_index("resp")
        self.y, self.z = prompt // SIDE, prompt % SIDE
        self.x, self.c = resp // 2, resp % 2
        self.prompt, self.resp = prompt, resp
        x, y, z, c = self.x, self.y, self.z, self.c
        self.sibling = (prompt, x * 2 + 1 - c)
        self.home_slot = 2 * (x * (1 - c) + y * c) + c
        self.head = x * (1 - c) + (SIDE + y) * c
        self.line = y * (1 - c) + x * c
        self.routes = []
        for k in (2, 1, 3):
            xd, yd = (x + k) % SIDE, (y + k) % SIDE
            self.routes.append((xd, 2 * x + c, (prompt, 2 * xd)))
            self.routes.append((SIDE + yd, 2 * y + c, (yd * SIDE + z, 2 * x + 1)))
        self.routes.append(((SIDE + y) * (1 - c) + x * c, 2 * y * (1 - c) + (2 * x + 1) * c, self.sibling))
        self.routes.append((self.head, self.home_slot, None))

    def source(self, k, core):
        along = (self.x * (1 - self.c) + self.y * self.c + k) % SIDE
        prompt = self.prompt * (1 - self.c) + (along * SIDE + self.z) * self.c
        resp = (along * 2 + core) * (1 - self.c) + (2 * self.x + core) * self.c
        return 2 * along + core, (prompt, resp)

    def line_peer(self, k):
        prompt = ((self.y + k * (1 - self.c)) % SIDE) * SIDE + self.z
        return (prompt, ((self.x + k * self.c) % SIDE) * 2 + self.c)

    def beside(self, n, k):
        x, y, z, c = self.x, self.y, self.z, self.c
        if n == 7:
            return self.line_peer(k)
        if n == 6:
            return (((y + k * c) % SIDE) * SIDE + z, ((x + k * (1 - c)) % SIDE) * 2 + 1 - c)
        ahead = (2, 1, 3)[n // 2]
        if n % 2 == 0:
            return (((y + k) % SIDE) * SIDE + z, 2 * ((x + ahead) % SIDE))
        return (((y + ahead) % SIDE) * SIDE + z, 2 * ((x + k) % SIDE) + 1)

    def z_peer(self, k):
        return (self.y * SIDE + (self.z + k) % SIDE, self.resp)

    def barrier(self):
        sem = pltpu.get_barrier_semaphore()
        peers = [self.sibling]
        for k in (1, 2, 3):
            peers.append(self.z_peer(k))
            for core in (0, 1):
                peers.append((self.prompt, ((self.x + k) % SIDE) * 2 + core))
                peers.append((((self.y + k) % SIDE) * SIDE + self.z, 2 * self.x + core))
                for j in (1, 2, 3):
                    peers.append((((self.y + k) % SIDE) * SIDE + self.z, ((self.x + j) % SIDE) * 2 + core))
        for peer in peers:
            pl.semaphore_signal(sem, inc=1, device_id=peer, device_id_type=MESH)
        pl.semaphore_wait(sem, len(peers))


def remote(src, dst, send, recv, device):
    return pltpu.make_async_remote_copy(
        src_ref=src, dst_ref=dst, send_sem=send, recv_sem=recv, device_id=device, device_id_type=MESH
    )


def pack_rows(len_ref, prm_ref):
    lane = lax.broadcasted_iota(jnp.int32, (1, TOKENS), 1)
    response, token = lane >> 4, lane & (SLOTS - 1)
    row = jnp.full((1, TOKENS), -1, jnp.int32)
    slot = jnp.zeros((1, TOKENS), jnp.int32)
    start = jnp.int32(0)
    for j in range(RESPONSES):
        length = len_ref[j]
        mine = response == j
        row = jnp.where(mine & (token < length), start + token, row)
        slot = jnp.where(mine, prm_ref[j] * SLOTS + token, slot)
        start = start + length
    return row, slot


def one_hot_pack(row):
    packed = lax.broadcasted_iota(jnp.int32, (LIVE, TOKENS), 0)
    return jnp.where(packed == row, 1.0, 0.0).astype(BF16)


def dot(a, b, dims):
    return lax.dot_general(a, b, (dims, ((), ())), preferred_element_type=F32)


NN = ((1,), (0,))
NT = ((1,), (1,))
TN = ((0,), (0,))


def main_kernel(
    len_ref, prm_ref, q, g, k, v, pk, pv, back, grads,
    xb, send, slot_send, recv, slots, kv, pkv, xu, ou, dkv, half_sum, got_m, got_p, plane_sum, got_y, got_x, final_y, final_x,
    in_sem, x_send, x_recv, sl_send, sl_recv, a_send, a_recv, b_send, b_recv,
    cp_send, cp_recv, cm_send, cm_recv, f_send, f_recv,
    h_send, h_recv, gm_send, gm_recv, gp_send, gp_recv, d_send, d_recv, e_send, e_recv, r_send, r_recv, own_sem,
):
    me = Place()
    routes = me.routes
    after, before = me.z_peer(1), me.z_peer(SIDE - 1)
    plane_of = lambda k: (me.z + k) % SIDE
    piece_of = lambda offset: (me.line + offset) % SIDE

    def core_rows(core):
        return pl.ds(pl.multiple_of(core * ROWS, 16), ROWS)

    def await_recv(ref, sem):
        remote(ref, ref, x_send.at[0], sem, me.sibling).wait_recv()

    def await_send(ref, sem):
        remote(ref, ref, sem, x_recv.at[0], me.sibling).wait_send()

    for n, (head, _, _) in enumerate(routes):
        wide = pl.ds(pl.multiple_of(head * GW, WIDTH), GW)
        narrow = pl.ds(pl.multiple_of(head * WIDTH, WIDTH), WIDTH)
        for src, cols, low, size in ((q, wide, 0, GW), (g, wide, GW, GW), (k, narrow, 2 * GW, WIDTH), (v, narrow, 2 * GW + WIDTH, WIDTH)):
            pltpu.make_async_copy(src.at[:, cols], xb.at[n, :, pl.ds(low, size)], in_sem.at[n]).start()
    for i, src in enumerate((pk, pv)):
        for h in range(KEY_HEADS):
            pltpu.make_async_copy(src.at[:, pl.ds(h * WIDTH, WIDTH)], pkv.at[h, i], own_sem.at[2]).start()
    me.barrier()
    pltpu.make_async_copy(pkv, pkv, own_sem.at[2]).wait()

    for k in (0, 1, 3, 2):
        for n, (head, there, device) in enumerate(routes):
            on_y = head // SIDE
            piece, part = me.y * (1 - on_y) + me.x * on_y, me.x * (1 - on_y) + me.y * on_y
            src, dst = pkv.at[head], kv.at[me.z, piece, part, :, core_rows(me.c)]
            if k > 0:
                remote(src, dst, b_send.at[k - 1], b_recv.at[k - 1], me.beside(n, k)).start()
            elif device is None:
                pltpu.make_async_copy(src, dst, own_sem.at[1]).start()
            else:
                remote(src, dst, a_send.at[n], a_recv.at[there], device).start()

    row, slot = pack_rows(len_ref, prm_ref)
    pack = one_hot_pack(row)
    slot8 = jnp.broadcast_to(slot, (8, TOKENS)).astype(F32).astype(BF16)
    slot_send[...] = dot(slot8, pack, NT)
    for n, (_, there, device) in enumerate(routes):
        if device is None:
            pltpu.make_async_copy(slot_send, slots.at[there], own_sem.at[3]).start()
        else:
            remote(slot_send, slots.at[there], sl_send.at[n], sl_recv.at[there], device).start()

    def pack_rows_of(n):
        _, there, device = routes[n]
        pltpu.make_async_copy(xb.at[n], xb.at[n], in_sem.at[n]).wait()
        rows = dot(pack, xb[n], NN).astype(BF16)
        if device is None:
            recv[there] = rows
        else:
            send[n] = rows

    def send_rows(n):
        _, there, device = routes[n]
        if device is not None:
            remote(send.at[n], recv.at[there], x_send.at[n], x_recv.at[there], device).start()

    def pass_on(offset, ahead, sem, device):
        ref = kv.at[plane_of(ahead), piece_of(offset)]
        await_recv(ref, sem.at[offset])
        remote(ref, ref, f_send.at[offset], f_recv.at[offset], device).start()

    def spread(offset):
        ref = kv.at[me.z, piece_of(offset)]
        remote(ref, ref, cp_send.at[offset], cp_recv.at[offset], after).start()
        remote(ref, ref, cm_send.at[offset], cm_recv.at[offset], before).start()

    for n in range(FIRST):
        pack_rows_of(n)
        send_rows(n)
    for k in range(SIDE):
        for core in (0, 1):
            there, _ = me.source(k, core)
            dst = kv.at[me.z, me.line, there // 2, :, core_rows(core)]
            if k == 0:
                pl.when(me.c == core)(lambda dst=dst: pltpu.make_async_copy(dst, dst, own_sem.at[1]).wait())
                pl.when(me.c != core)(lambda dst=dst, there=there: await_recv(dst, a_recv.at[there]))
            else:
                await_recv(dst, a_recv.at[there])
    spread(0)
    for n in range(FIRST, 4):
        pack_rows_of(n)
        send_rows(n)
    for k in (1, 3, 2):
        await_recv(kv.at[me.z, piece_of(k)], b_recv.at[SIDE - k - 1])
        spread(k)
        n = {1: 4, 3: 5, 2: 6}[k]
        pack_rows_of(n)
        send_rows(n)
    pack_rows_of(7)
    pass_on(0, 3, cp_recv, after)
    pass_on(1, 3, cp_recv, after)
    pass_on(3, 1, cm_recv, before)
    pass_on(2, 1, cm_recv, before)
    def one_hot(i):
        slot = slots[i][0:1].astype(jnp.int32)
        return jnp.where(lax.broadcasted_iota(jnp.int32, (TOKENS, LIVE), 0) == slot, 1.0, 0.0).astype(BF16)

    pltpu.make_async_copy(slot_send, slots.at[me.home_slot], own_sem.at[3]).wait()

    def unpack(m, carry):
        ahead = 2 + m // 2 + m // 4 + 2 * (m // 6)
        there = 2 * ((me.home_slot // 2 + ahead) % SIDE) + m % 2

        @pl.when(there != me.home_slot)
        def _():
            await_recv(slots.at[there], sl_recv.at[there])
            await_recv(recv.at[there], x_recv.at[there])

        rows = dot(one_hot(there), recv[there], NN).astype(BF16)
        xu[:, pl.ds(pl.multiple_of(there * SLOTS, SLOTS), SLOTS), :] = rows.reshape(RESPONSES, SLOTS, MSG)
        return carry

    lax.fori_loop(0, 8, unpack, 0)
    own_rows = lax.broadcasted_iota(jnp.int32, (WIDTH, WIDTH), 0)
    own_cols = lax.broadcasted_iota(jnp.int32, (WIDTH, WIDTH), 1)
    own_mask = (own_rows >> 4 == own_cols >> 4) & (own_cols <= own_rows)
    own_mask = jnp.concatenate([own_mask] * GROUP, axis=0)
    c = me.c

    def prompt(gz, gy):
        number = gy * SIDE + gz

        def chunk(i, quarter):
            return gz, gy * (1 - c) + quarter * c, quarter * (1 - c) + gy * c, i

        def heads(low):
            return jnp.concatenate([xu[number, :, low + a * WIDTH : low + (a + 1) * WIDTH] for a in range(GROUP)], axis=0)

        def put(low, rows):
            ou[:, gz, pl.ds(pl.multiple_of(gy * SLOTS, SLOTS), SLOTS), low : low + WIDTH] = rows.reshape(8, SLOTS, WIDTH)

        queries, grad_rows = heads(0), heads(GW)
        keys = jnp.concatenate([kv[chunk(0, i)] for i in range(SIDE)] + [xu[number, :, 2 * GW : 2 * GW + WIDTH]], axis=0)
        values = jnp.concatenate([kv[chunk(1, i)] for i in range(SIDE)] + [xu[number, :, 2 * GW + WIDTH :]], axis=0)
        scores = dot(queries, keys, NT)
        scores = jnp.concatenate([scores[:, :PREFIX], jnp.where(own_mask, scores[:, PREFIX:], -1e30)], axis=1)
        top = jnp.max(scores, axis=1, keepdims=True)
        weights = jnp.exp2((scores - top) * EXP2_SCALE)
        over = 1.0 / jnp.sum(weights, axis=1, keepdims=True)
        half = weights.astype(BF16)
        out = dot(half, values, NN) * over
        scaled = (grad_rows.astype(F32) * over).astype(BF16)
        row_dot = jnp.sum(scaled.astype(F32) * out, axis=1, keepdims=True)
        score_grad = (weights * (dot(scaled, values, NT) - row_dot)).astype(BF16)
        query_grad = dot(score_grad, keys, NN) * SCALE
        key_grad = (dot(score_grad, queries, TN) * SCALE).astype(BF16)
        value_grad = dot(half, scaled, TN).astype(BF16)
        dkv[gz, gy, 0] = key_grad[:PREFIX]
        dkv[gz, gy, 1] = value_grad[:PREFIX]
        for a in range(GROUP):
            put(a * WIDTH, out[a * WIDTH : (a + 1) * WIDTH].astype(BF16))
            put(GW + a * WIDTH, query_grad[a * WIDTH : (a + 1) * WIDTH].astype(BF16))
        put(2 * GW, key_grad[PREFIX:])
        put(2 * GW + WIDTH, value_grad[PREFIX:])

    def send_back(gz, gy):
        rows = pl.ds(pl.multiple_of(gy * SLOTS, SLOTS), SLOTS)
        for k in (2, 1, 3, 0):
            for core in (0, 1):
                there, device = me.source(k, core)
                index = 2 * k + core
                src, dst = ou.at[there, gz, rows], back.at[me.head, gz, rows]
                away = lambda: remote(src, dst, r_send.at[index], r_recv.at[me.head], device).start()
                if k == 0:
                    pl.when(c == core)(lambda: pltpu.make_async_copy(src, dst, own_sem.at[0]).start())
                    pl.when(c != core)(away)
                else:
                    away()

    def plan(n):
        quarter, odd = n // 4, n % 2
        first, middle = 1 - (quarter + 3) // 4, (quarter * (3 - quarter)) // 2
        ahead = first * 2 + middle * (1 + 2 * odd)
        gy = first * (odd * 2 + n // 2) + middle * (((n + 4) // 2 + 2 * (1 - odd)) % SIDE) + (1 - first - middle) * (n % SIDE)
        return (me.z + ahead) % SIDE, gy

    def step(count, carry):
        n = (count + SHIFT) % RESPONSES
        gz, gy = plan(n)

        @pl.when(n == 0)
        def _():
            for offset in (0, 3, 1, 2):
                await_recv(kv.at[plane_of(2), piece_of(offset)], f_recv.at[offset])

        @pl.when(n == 4)
        def _():
            for offset in (0, 1):
                await_recv(kv.at[plane_of(1), piece_of(offset)], cm_recv.at[offset])
            for offset in (3, 2):
                await_recv(kv.at[plane_of(3), piece_of(offset)], cp_recv.at[offset])

        prompt(gz, gy)

        @pl.when((n >= 8) & (n < 12))
        def _():
            await_recv(half_sum.at[gy], h_recv.at[gy])
            dkv[gz, gy] = (dkv[gz, gy].astype(F32) + half_sum[gy].astype(F32)).astype(BF16)

        for odd, device, got, send_sem, recv_sem in ((0, after, got_m, gm_send, gm_recv), (1, before, got_p, gp_send, gp_recv)):

            @pl.when((n < 4) & (n % 2 == odd))
            def _():
                remote(dkv.at[gz, gy], half_sum.at[gy], h_send.at[gy], h_recv.at[gy], device).start()

            @pl.when((n >= 4) & (n < 12) & (n % 2 == odd))
            def _():
                remote(dkv.at[gz, gy], got.at[gy], send_sem.at[gy], recv_sem.at[gy], device).start()

        @pl.when(count < HOLD)
        def _():
            send_back(gz, gy)

        return carry

    lax.fori_loop(0, RESPONSES, step, 0)

    def add_up(gy, carry):
        await_recv(got_m.at[gy], gm_recv.at[gy])
        await_recv(got_p.at[gy], gp_recv.at[gy])
        total = dkv[me.z, gy].astype(F32) + got_m[gy].astype(F32) + got_p[gy].astype(F32)
        plane_sum[gy] = total.astype(BF16)
        return carry

    lax.fori_loop(0, SIDE, add_up, 0)

    def columns(k):
        return pl.ds(pl.multiple_of((me.x + k) % SIDE * 96, 16), 96)

    @pl.when(c == 0)
    def _():
        for k in (2, 1, 3):
            remote(plane_sum.at[(me.y + k) % SIDE], got_y.at[k - 1], d_send.at[k - 1], d_recv.at[k - 1], me.line_peer(k)).start()

    @pl.when(c != 0)
    def _():
        for k in (2, 1, 3):
            remote(plane_sum.at[:, :, columns(k)], got_x.at[k - 1], d_send.at[k - 1], d_recv.at[k - 1], me.line_peer(k)).start()

    def late(n, carry):
        send_back(*plan((n + SHIFT) % RESPONSES))
        return carry

    lax.fori_loop(HOLD, RESPONSES, late, 0)

    def send_grads(part):
        for k in (2, 1, 3, 0):
            for core in (0, 1):
                _, device = me.source(k, core)
                index = 2 * k + core
                src, dst = part(k, core), grads.at[me.head]
                if k > 0 or core == 1 - part.core:
                    remote(src, dst, e_send.at[index], e_recv.at[me.head], device).start()
                else:
                    pltpu.make_async_copy(src, dst, own_sem.at[1]).start()

    @pl.when(c == 0)
    def _():
        total = plane_sum[me.y].astype(F32)
        for k in (1, 3, 2):
            await_recv(got_y.at[k - 1], d_recv.at[k - 1])
            total = total + got_y[k - 1].astype(F32)
        final_y[...] = total.astype(BF16)

        def part(k, core):
            return final_y.at[:, pl.ds(pl.multiple_of((2 * ((me.x + k) % SIDE) + core) * ROWS, 16), ROWS)]

        part.core = 0
        send_grads(part)

    @pl.when(c != 0)
    def _():
        total = plane_sum[:, :, columns(0)].astype(F32)
        for k in (1, 3, 2):
            await_recv(got_x.at[k - 1], d_recv.at[k - 1])
            total = total + got_x[k - 1].astype(F32)
        final_x[...] = total.astype(BF16)

        def part(k, core):
            return final_x.at[(me.y + k) % SIDE, :, pl.ds(core * ROWS, ROWS)]

        part.core = 1
        send_grads(part)

    for head, _, device in routes:
        if device is None:
            pltpu.make_async_copy(back.at[head], back.at[head], own_sem.at[0]).wait()
            pltpu.make_async_copy(grads.at[head], grads.at[head], own_sem.at[1]).wait()
        else:
            await_recv(back.at[head], r_recv.at[head])
            await_recv(grads.at[head], e_recv.at[head])
    for n in range(7):
        await_send(send.at[n], x_send.at[n])
        await_send(slot_send, sl_send.at[n])
        await_send(grads.at[0], a_send.at[n])
    for k in range(3):
        await_send(got_y.at[k], b_send.at[k])
        await_send(got_y.at[k], d_send.at[k])
    for offset in range(SIDE):
        for sem in (cp_send, cm_send, f_send, h_send, gm_send, gp_send):
            await_send(got_m.at[offset], sem.at[offset])

    def sent_back(index):
        await_send(back.at[0], r_send.at[index])
        await_send(grads.at[0], e_send.at[index])

    for index in range(8):
        if index < 2:
            pl.when(c != index)(lambda: sent_back(index))
        else:
            sent_back(index)


def place_kernel(len_ref, prm_ref, *refs):
    blocks, (grads, attn, query, key, value, prefix_key, prefix_value) = refs[:BATCH], refs[BATCH:]
    step = pl.program_id(0)
    token = lax.broadcasted_iota(jnp.int32, (SLOTS, GW), 0)
    for m, block in enumerate(blocks):
        live = token < len_ref[step * BATCH + m]
        rows = slice(m * SLOTS, (m + 1) * SLOTS)
        for h in range(KEY_HEADS):
            attn[rows, h * GW : (h + 1) * GW] = jnp.where(live, block[h, 0, :, :GW], jnp.zeros((), BF16))
            query[rows, h * GW : (h + 1) * GW] = block[h, 0, :, GW : 2 * GW]
            key[rows, h * WIDTH : (h + 1) * WIDTH] = block[h, 0, :, 2 * GW : 2 * GW + WIDTH]
            value[rows, h * WIDTH : (h + 1) * WIDTH] = block[h, 0, :, 2 * GW + WIDTH :]

    @pl.when(step == 0)
    def _():
        for h in range(KEY_HEADS):
            prefix_key[:, h * WIDTH : (h + 1) * WIDTH] = grads[h, 0].astype(F32)
            prefix_value[:, h * WIDTH : (h + 1) * WIDTH] = grads[h, 1].astype(F32)


def spec(space):
    return pl.BlockSpec(memory_space=space)


DMA = pltpu.SemaphoreType.DMA


def local(queries, grad_out, response_keys, response_values, prompt_prefix_keys, prompt_prefix_values, lengths, prompt_of):
    q, g = queries.reshape(TOKENS, KEY_HEADS * GW), grad_out.reshape(TOKENS, KEY_HEADS * GW)
    k, v = response_keys.reshape(TOKENS, KEY_HEADS * WIDTH), response_values.reshape(TOKENS, KEY_HEADS * WIDTH)
    pk, pv = prompt_prefix_keys.reshape(ROWS, KEY_HEADS * WIDTH), prompt_prefix_values.reshape(ROWS, KEY_HEADS * WIDTH)
    lens, prompts = lengths.reshape(RESPONSES), prompt_of.reshape(RESPONSES)
    vmem = pltpu.VMEM
    back, grads = pl.pallas_call(
        main_kernel,
        out_shape=(
            jax.ShapeDtypeStruct((8, SIDE, SIDE * SLOTS, MSG), BF16),
            jax.ShapeDtypeStruct((8, 2, ROWS, WIDTH), BF16),
        ),
        in_specs=[spec(pltpu.SMEM)] * 2 + [spec(pl.ANY)] * 6,
        out_specs=(spec(pl.ANY),) * 2,
        scratch_shapes=[
            vmem((8, TOKENS, MSG), BF16), vmem((7, LIVE, MSG), BF16), vmem((8, LIVE), F32),
            vmem((8, LIVE, MSG), BF16), vmem((8, 8, LIVE), F32), vmem((SIDE, SIDE, SIDE, 2, 96, WIDTH), BF16),
            vmem((KEY_HEADS, 2, ROWS, WIDTH), BF16),
            vmem((RESPONSES, 8 * SLOTS, MSG), BF16), vmem((8, SIDE, SIDE * SLOTS, MSG), BF16),
            vmem((SIDE, SIDE, 2, PREFIX, WIDTH), BF16), vmem((SIDE, 2, PREFIX, WIDTH), BF16), vmem((SIDE, 2, PREFIX, WIDTH), BF16),
            vmem((SIDE, 2, PREFIX, WIDTH), BF16), vmem((SIDE, 2, PREFIX, WIDTH), BF16),
            vmem((3, 2, PREFIX, WIDTH), BF16), vmem((3, SIDE, 2, 96, WIDTH), BF16),
            vmem((2, PREFIX, WIDTH), BF16), vmem((SIDE, 2, 96, WIDTH), BF16),
            DMA((8,)), DMA((8,)), DMA((8,)), DMA((8,)), DMA((8,)), DMA((8,)), DMA((8,)), DMA((3,)), DMA((3,)),
        ] + [DMA((SIDE,))] * 12 + [DMA((3,)), DMA((3,)), DMA((8,)), DMA((8,)), DMA((8,)), DMA((8,)), DMA((4,))],
        compiler_params=pltpu.CompilerParams(collective_id=0, has_side_effects=True, vmem_limit_bytes=VMEM_LIMIT),
    )(lens, prompts, q, g, k, v, pk, pv)
    def block_of(m):
        def index(i, lens, prompts):
            there = prompts[i * BATCH + m]
            return 0, there % SIDE, there // SIDE, 0

        return pl.BlockSpec((KEY_HEADS, 1, SLOTS, MSG), index)

    wide = pl.BlockSpec((BATCH * SLOTS, KEY_HEADS * GW), lambda i, *_: (i, 0))
    narrow = pl.BlockSpec((BATCH * SLOTS, KEY_HEADS * WIDTH), lambda i, *_: (i, 0))
    prefix = pl.BlockSpec((ROWS, KEY_HEADS * WIDTH), lambda i, *_: (0, 0))
    outs = pl.pallas_call(
        place_kernel,
        grid_spec=pltpu.PrefetchScalarGridSpec(
            num_scalar_prefetch=2,
            grid=(RESPONSES // BATCH,),
            in_specs=[block_of(m) for m in range(BATCH)] + [pl.BlockSpec(grads.shape, lambda i, *_: (0, 0, 0, 0))],
            out_specs=[wide, wide, narrow, narrow, prefix, prefix],
        ),
        out_shape=[
            jax.ShapeDtypeStruct(q.shape, BF16),
            jax.ShapeDtypeStruct(q.shape, BF16),
            jax.ShapeDtypeStruct(k.shape, BF16),
            jax.ShapeDtypeStruct(k.shape, BF16),
            jax.ShapeDtypeStruct(pk.shape, F32),
            jax.ShapeDtypeStruct(pk.shape, F32),
        ],
        compiler_params=pltpu.CompilerParams(vmem_limit_bytes=VMEM_LIMIT),
    )(lens, prompts, *[back] * BATCH, grads)
    shapes = (queries, queries, response_keys, response_keys, prompt_prefix_keys, prompt_prefix_keys)
    return tuple(out.reshape(like.shape) for out, like in zip(outs, shapes))


def solution(mesh):
    five, three = P("prompt", "resp", None, None, None), P("prompt", "resp", None)
    return jax.shard_map(
        local,
        mesh=mesh,
        in_specs=(five, five, five, five, three, three, three, three),
        out_specs=(five, five, five, five, three, three),
        check_vma=False,
    )
```

```python
import jax
import jax.numpy as jnp
from jax import lax
from jax.experimental import pallas as pl
from jax.experimental.pallas import tpu as pltpu
from jax.sharding import PartitionSpec as P

KEY_HEADS = 8
WIDTH = 128
GROUP = 5
SLOTS = 16
RESPONSES = 16
TOKENS = SLOTS * RESPONSES
LIVE = 160
PREFIX = 384
SIDE = 4
ROWS = PREFIX // 8
GW = GROUP * WIDTH
MSG = 2 * GW + 2 * WIDTH
MESH = pl.DeviceIdType.MESH
BF16 = jnp.bfloat16
F32 = jnp.float32
SCALE = WIDTH**-0.5
EXP2_SCALE = SCALE * 1.4426950408889634
BATCH = 8
HOLD = 14
FIRST = 2
LOW, HIGH, BOTH = pl.ds(0, 2), pl.ds(2, 2), pl.ds(0, 4)
PASSED = ((0, LOW), (0, HIGH), (1, BOTH), (3, BOTH), (2, LOW), (2, HIGH))
SHIFT = 0
VMEM_LIMIT = 58 * 1024 * 1024


class Place:
    def __init__(self):
        prompt, resp = lax.axis_index("prompt"), lax.axis_index("resp")
        self.y, self.z = prompt // SIDE, prompt % SIDE
        self.x, self.c = resp // 2, resp % 2
        self.prompt, self.resp = prompt, resp
        x, y, z, c = self.x, self.y, self.z, self.c
        self.sibling = (prompt, x * 2 + 1 - c)
        self.home_slot = 2 * (x * (1 - c) + y * c) + c
        self.head = x * (1 - c) + (SIDE + y) * c
        self.line = y * (1 - c) + x * c
        self.routes = []
        for k in (2, 1, 3):
            xd, yd = (x + k) % SIDE, (y + k) % SIDE
            self.routes.append((xd, 2 * x + c, (prompt, 2 * xd)))
            self.routes.append((SIDE + yd, 2 * y + c, (yd * SIDE + z, 2 * x + 1)))
        self.routes.append(((SIDE + y) * (1 - c) + x * c, 2 * y * (1 - c) + (2 * x + 1) * c, self.sibling))
        self.routes.append((self.head, self.home_slot, None))

    def source(self, k, core):
        along = (self.x * (1 - self.c) + self.y * self.c + k) % SIDE
        prompt = self.prompt * (1 - self.c) + (along * SIDE + self.z) * self.c
        resp = (along * 2 + core) * (1 - self.c) + (2 * self.x + core) * self.c
        return 2 * along + core, (prompt, resp)

    def line_peer(self, k):
        prompt = ((self.y + k * (1 - self.c)) % SIDE) * SIDE + self.z
        return (prompt, ((self.x + k * self.c) % SIDE) * 2 + self.c)

    def beside(self, n, k):
        x, y, z, c = self.x, self.y, self.z, self.c
        if n == 7:
            return self.line_peer(k)
        if n == 6:
            return (((y + k * c) % SIDE) * SIDE + z, ((x + k * (1 - c)) % SIDE) * 2 + 1 - c)
        ahead = (2, 1, 3)[n // 2]
        if n % 2 == 0:
            return (((y + k) % SIDE) * SIDE + z, 2 * ((x + ahead) % SIDE))
        return (((y + ahead) % SIDE) * SIDE + z, 2 * ((x + k) % SIDE) + 1)

    def z_peer(self, k):
        return (self.y * SIDE + (self.z + k) % SIDE, self.resp)

    def barrier(self):
        sem = pltpu.get_barrier_semaphore()
        peers = [self.sibling]
        for k in (1, 2, 3):
            peers.append(self.z_peer(k))
            for core in (0, 1):
                peers.append((self.prompt, ((self.x + k) % SIDE) * 2 + core))
                peers.append((((self.y + k) % SIDE) * SIDE + self.z, 2 * self.x + core))
                for j in (1, 2, 3):
                    peers.append((((self.y + k) % SIDE) * SIDE + self.z, ((self.x + j) % SIDE) * 2 + core))
        for peer in peers:
            pl.semaphore_signal(sem, inc=1, device_id=peer, device_id_type=MESH)
        pl.semaphore_wait(sem, len(peers))


def remote(src, dst, send, recv, device):
    return pltpu.make_async_remote_copy(
        src_ref=src, dst_ref=dst, send_sem=send, recv_sem=recv, device_id=device, device_id_type=MESH
    )


def pack_rows(len_ref, prm_ref):
    lane = lax.broadcasted_iota(jnp.int32, (1, TOKENS), 1)
    response, token = lane >> 4, lane & (SLOTS - 1)
    row = jnp.full((1, TOKENS), -1, jnp.int32)
    slot = jnp.zeros((1, TOKENS), jnp.int32)
    start = jnp.int32(0)
    for j in range(RESPONSES):
        length = len_ref[j]
        mine = response == j
        row = jnp.where(mine & (token < length), start + token, row)
        slot = jnp.where(mine, prm_ref[j] * SLOTS + token, slot)
        start = start + length
    return row, slot


def one_hot_pack(row):
    packed = lax.broadcasted_iota(jnp.int32, (LIVE, TOKENS), 0)
    return jnp.where(packed == row, 1.0, 0.0).astype(BF16)


def dot(a, b, dims):
    return lax.dot_general(a, b, (dims, ((), ())), preferred_element_type=F32)


NN = ((1,), (0,))
NT = ((1,), (1,))
TN = ((0,), (0,))


def main_kernel(
    len_ref, prm_ref, q, g, k, v, pk, pv, back, grads,
    xb, send, slot_send, recv, slots, kv, pkv, xu, ou, dkv, half_sum, got_m, got_p, plane_sum, got_y, got_x, final_y, final_x,
    in_sem, x_send, x_recv, sl_send, sl_recv, a_send, a_recv, b_send, b_recv,
    cp_send, cp_recv, cm_send, cm_recv, f_send, f_recv,
    h_send, h_recv, gm_send, gm_recv, gp_send, gp_recv, d_send, d_recv, e_send, e_recv, r_send, r_recv, own_sem,
):
    me = Place()
    routes = me.routes
    after, before = me.z_peer(1), me.z_peer(SIDE - 1)
    plane_of = lambda k: (me.z + k) % SIDE
    piece_of = lambda offset: (me.line + offset) % SIDE

    def core_rows(core):
        return pl.ds(pl.multiple_of(core * ROWS, 16), ROWS)

    def await_recv(ref, sem):
        remote(ref, ref, x_send.at[0], sem, me.sibling).wait_recv()

    def await_send(ref, sem):
        remote(ref, ref, sem, x_recv.at[0], me.sibling).wait_send()

    for n, (head, _, _) in enumerate(routes):
        wide = pl.ds(pl.multiple_of(head * GW, WIDTH), GW)
        narrow = pl.ds(pl.multiple_of(head * WIDTH, WIDTH), WIDTH)
        for src, cols, low, size in ((q, wide, 0, GW), (g, wide, GW, GW), (k, narrow, 2 * GW, WIDTH), (v, narrow, 2 * GW + WIDTH, WIDTH)):
            pltpu.make_async_copy(src.at[:, cols], xb.at[n, :, pl.ds(low, size)], in_sem.at[n]).start()
    for i, src in enumerate((pk, pv)):
        for h in range(KEY_HEADS):
            pltpu.make_async_copy(src.at[:, pl.ds(h * WIDTH, WIDTH)], pkv.at[h, i], own_sem.at[2]).start()
    me.barrier()
    pltpu.make_async_copy(pkv, pkv, own_sem.at[2]).wait()

    for k in (0, 1, 3, 2):
        for n, (head, there, device) in enumerate(routes):
            on_y = head // SIDE
            piece, part = me.y * (1 - on_y) + me.x * on_y, me.x * (1 - on_y) + me.y * on_y
            src, dst = pkv.at[head], kv.at[me.z, piece, part, :, core_rows(me.c)]
            if k > 0:
                remote(src, dst, b_send.at[k - 1], b_recv.at[k - 1], me.beside(n, k)).start()
            elif device is None:
                pltpu.make_async_copy(src, dst, own_sem.at[1]).start()
            else:
                remote(src, dst, a_send.at[n], a_recv.at[there], device).start()

    row, slot = pack_rows(len_ref, prm_ref)
    pack = one_hot_pack(row)
    slot8 = jnp.broadcast_to(slot, (8, TOKENS)).astype(F32).astype(BF16)
    slot_send[...] = dot(slot8, pack, NT)
    for n, (_, there, device) in enumerate(routes):
        if device is None:
            pltpu.make_async_copy(slot_send, slots.at[there], own_sem.at[3]).start()
        else:
            remote(slot_send, slots.at[there], sl_send.at[n], sl_recv.at[there], device).start()

    def pack_rows_of(n):
        _, there, device = routes[n]
        pltpu.make_async_copy(xb.at[n], xb.at[n], in_sem.at[n]).wait()
        rows = dot(pack, xb[n], NN).astype(BF16)
        if device is None:
            recv[there] = rows
        else:
            send[n] = rows

    def send_rows(n):
        _, there, device = routes[n]
        if device is not None:
            remote(send.at[n], recv.at[there], x_send.at[n], x_recv.at[there], device).start()

    def pass_on(offset, index, parts, forward):
        ref = kv.at[plane_of(3 if forward else 1), piece_of(offset)]
        await_recv(ref, (cp_recv if forward else cm_recv).at[offset])
        ref = ref.at[parts]
        remote(ref, ref, f_send.at[index], f_recv.at[index], after if forward else before).start()

    def spread(offset):
        ref = kv.at[me.z, piece_of(offset)]
        remote(ref, ref, cp_send.at[offset], cp_recv.at[offset], after).start()
        remote(ref, ref, cm_send.at[offset], cm_recv.at[offset], before).start()

    for n in range(FIRST):
        pack_rows_of(n)
        send_rows(n)
    for k in range(SIDE):
        for core in (0, 1):
            there, _ = me.source(k, core)
            dst = kv.at[me.z, me.line, there // 2, :, core_rows(core)]
            if k == 0:
                pl.when(me.c == core)(lambda dst=dst: pltpu.make_async_copy(dst, dst, own_sem.at[1]).wait())
                pl.when(me.c != core)(lambda dst=dst, there=there: await_recv(dst, a_recv.at[there]))
            else:
                await_recv(dst, a_recv.at[there])
    spread(0)
    for n in range(FIRST, 4):
        pack_rows_of(n)
        send_rows(n)
    pass_on(0, 0, LOW, True)
    pass_on(0, 1, HIGH, False)
    for k in (1, 3, 2):
        await_recv(kv.at[me.z, piece_of(k)], b_recv.at[SIDE - k - 1])
        spread(k)
        n = {1: 4, 3: 5, 2: 6}[k]
        pack_rows_of(n)
        send_rows(n)
    pack_rows_of(7)
    pass_on(1, 2, BOTH, True)
    pass_on(3, 3, BOTH, False)
    pass_on(2, 4, LOW, True)
    pass_on(2, 5, HIGH, False)

    def one_hot(i):
        slot = slots[i][0:1].astype(jnp.int32)
        return jnp.where(lax.broadcasted_iota(jnp.int32, (TOKENS, LIVE), 0) == slot, 1.0, 0.0).astype(BF16)

    pltpu.make_async_copy(slot_send, slots.at[me.home_slot], own_sem.at[3]).wait()

    def unpack(m, carry):
        ahead = 2 + m // 2 + m // 4 + 2 * (m // 6)
        there = 2 * ((me.home_slot // 2 + ahead) % SIDE) + m % 2

        @pl.when(there != me.home_slot)
        def _():
            await_recv(slots.at[there], sl_recv.at[there])
            await_recv(recv.at[there], x_recv.at[there])

        rows = dot(one_hot(there), recv[there], NN).astype(BF16)
        xu[:, pl.ds(pl.multiple_of(there * SLOTS, SLOTS), SLOTS), :] = rows.reshape(RESPONSES, SLOTS, MSG)
        return carry

    lax.fori_loop(0, 8, unpack, 0)
    own_rows = lax.broadcasted_iota(jnp.int32, (WIDTH, WIDTH), 0)
    own_cols = lax.broadcasted_iota(jnp.int32, (WIDTH, WIDTH), 1)
    own_mask = (own_rows >> 4 == own_cols >> 4) & (own_cols <= own_rows)
    own_mask = jnp.concatenate([own_mask] * GROUP, axis=0)
    c = me.c

    def prompt(gz, gy):
        number = gy * SIDE + gz

        def chunk(i, quarter):
            return gz, gy * (1 - c) + quarter * c, quarter * (1 - c) + gy * c, i

        def heads(low):
            return jnp.concatenate([xu[number, :, low + a * WIDTH : low + (a + 1) * WIDTH] for a in range(GROUP)], axis=0)

        def put(low, rows):
            ou[:, gz, pl.ds(pl.multiple_of(gy * SLOTS, SLOTS), SLOTS), low : low + WIDTH] = rows.reshape(8, SLOTS, WIDTH)

        queries, grad_rows = heads(0), heads(GW)
        keys = jnp.concatenate([kv[chunk(0, i)] for i in range(SIDE)] + [xu[number, :, 2 * GW : 2 * GW + WIDTH]], axis=0)
        values = jnp.concatenate([kv[chunk(1, i)] for i in range(SIDE)] + [xu[number, :, 2 * GW + WIDTH :]], axis=0)
        scores = dot(queries, keys, NT)
        scores = jnp.concatenate([scores[:, :PREFIX], jnp.where(own_mask, scores[:, PREFIX:], -1e30)], axis=1)
        top = jnp.max(scores, axis=1, keepdims=True)
        weights = jnp.exp2((scores - top) * EXP2_SCALE)
        over = 1.0 / jnp.sum(weights, axis=1, keepdims=True)
        half = weights.astype(BF16)
        out = dot(half, values, NN) * over
        scaled = (grad_rows.astype(F32) * over).astype(BF16)
        row_dot = jnp.sum(scaled.astype(F32) * out, axis=1, keepdims=True)
        score_grad = (weights * (dot(scaled, values, NT) - row_dot)).astype(BF16)
        query_grad = dot(score_grad, keys, NN) * SCALE
        key_grad = (dot(score_grad, queries, TN) * SCALE).astype(BF16)
        value_grad = dot(half, scaled, TN).astype(BF16)
        dkv[gz, gy, 0] = key_grad[:PREFIX]
        dkv[gz, gy, 1] = value_grad[:PREFIX]
        for a in range(GROUP):
            put(a * WIDTH, out[a * WIDTH : (a + 1) * WIDTH].astype(BF16))
            put(GW + a * WIDTH, query_grad[a * WIDTH : (a + 1) * WIDTH].astype(BF16))
        put(2 * GW, key_grad[PREFIX:])
        put(2 * GW + WIDTH, value_grad[PREFIX:])

    def send_back(gz, gy):
        rows = pl.ds(pl.multiple_of(gy * SLOTS, SLOTS), SLOTS)
        for k in (2, 1, 3, 0):
            for core in (0, 1):
                there, device = me.source(k, core)
                index = 2 * k + core
                src, dst = ou.at[there, gz, rows], back.at[me.head, gz, rows]
                away = lambda: remote(src, dst, r_send.at[index], r_recv.at[me.head], device).start()
                if k == 0:
                    pl.when(c == core)(lambda: pltpu.make_async_copy(src, dst, own_sem.at[0]).start())
                    pl.when(c != core)(away)
                else:
                    away()

    def plan(n):
        quarter, odd = n // 4, n % 2
        first, middle = 1 - (quarter + 3) // 4, (quarter * (3 - quarter)) // 2
        ahead = first * 2 + middle * (1 + 2 * odd)
        gy = first * (odd * 2 + n // 2) + middle * (((n + 4) // 2 + 2 * (1 - odd)) % SIDE) + (1 - first - middle) * (n % SIDE)
        return (me.z + ahead) % SIDE, gy

    def step(count, carry):
        n = (count + SHIFT) % RESPONSES
        gz, gy = plan(n)

        @pl.when(n == 0)
        def _():
            for index, (offset, parts) in enumerate(PASSED):
                await_recv(kv.at[plane_of(2), piece_of(offset), parts], f_recv.at[index])

        @pl.when(n == 4)
        def _():
            await_recv(kv.at[plane_of(1), piece_of(1)], cm_recv.at[1])
            await_recv(kv.at[plane_of(3), piece_of(3)], cp_recv.at[3])

        prompt(gz, gy)

        @pl.when((n >= 8) & (n < 12))
        def _():
            await_recv(half_sum.at[gy], h_recv.at[gy])
            dkv[gz, gy] = (dkv[gz, gy].astype(F32) + half_sum[gy].astype(F32)).astype(BF16)

        for odd, device, got, send_sem, recv_sem in ((0, after, got_m, gm_send, gm_recv), (1, before, got_p, gp_send, gp_recv)):

            @pl.when((n < 4) & (n % 2 == odd))
            def _():
                remote(dkv.at[gz, gy], half_sum.at[gy], h_send.at[gy], h_recv.at[gy], device).start()

            @pl.when((n >= 4) & (n < 12) & (n % 2 == odd))
            def _():
                remote(dkv.at[gz, gy], got.at[gy], send_sem.at[gy], recv_sem.at[gy], device).start()

        @pl.when(count < HOLD)
        def _():
            send_back(gz, gy)

        return carry

    lax.fori_loop(0, RESPONSES, step, 0)

    def add_up(gy, carry):
        await_recv(got_m.at[gy], gm_recv.at[gy])
        await_recv(got_p.at[gy], gp_recv.at[gy])
        total = dkv[me.z, gy].astype(F32) + got_m[gy].astype(F32) + got_p[gy].astype(F32)
        plane_sum[gy] = total.astype(BF16)
        return carry

    lax.fori_loop(0, SIDE, add_up, 0)

    def columns(k):
        return pl.ds(pl.multiple_of((me.x + k) % SIDE * 96, 16), 96)

    @pl.when(c == 0)
    def _():
        for k in (2, 1, 3):
            remote(plane_sum.at[(me.y + k) % SIDE], got_y.at[k - 1], d_send.at[k - 1], d_recv.at[k - 1], me.line_peer(k)).start()

    @pl.when(c != 0)
    def _():
        for k in (2, 1, 3):
            remote(plane_sum.at[:, :, columns(k)], got_x.at[k - 1], d_send.at[k - 1], d_recv.at[k - 1], me.line_peer(k)).start()

    def late(n, carry):
        send_back(*plan((n + SHIFT) % RESPONSES))
        return carry

    lax.fori_loop(HOLD, RESPONSES, late, 0)

    def send_grads(part):
        for k in (2, 1, 3, 0):
            for core in (0, 1):
                _, device = me.source(k, core)
                index = 2 * k + core
                src, dst = part(k, core), grads.at[me.head]
                if k > 0 or core == 1 - part.core:
                    remote(src, dst, e_send.at[index], e_recv.at[me.head], device).start()
                else:
                    pltpu.make_async_copy(src, dst, own_sem.at[1]).start()

    @pl.when(c == 0)
    def _():
        total = plane_sum[me.y].astype(F32)
        for k in (1, 3, 2):
            await_recv(got_y.at[k - 1], d_recv.at[k - 1])
            total = total + got_y[k - 1].astype(F32)
        final_y[...] = total.astype(BF16)

        def part(k, core):
            return final_y.at[:, pl.ds(pl.multiple_of((2 * ((me.x + k) % SIDE) + core) * ROWS, 16), ROWS)]

        part.core = 0
        send_grads(part)

    @pl.when(c != 0)
    def _():
        total = plane_sum[:, :, columns(0)].astype(F32)
        for k in (1, 3, 2):
            await_recv(got_x.at[k - 1], d_recv.at[k - 1])
            total = total + got_x[k - 1].astype(F32)
        final_x[...] = total.astype(BF16)

        def part(k, core):
            return final_x.at[(me.y + k) % SIDE, :, pl.ds(core * ROWS, ROWS)]

        part.core = 1
        send_grads(part)

    for head, _, device in routes:
        if device is None:
            pltpu.make_async_copy(back.at[head], back.at[head], own_sem.at[0]).wait()
            pltpu.make_async_copy(grads.at[head], grads.at[head], own_sem.at[1]).wait()
        else:
            await_recv(back.at[head], r_recv.at[head])
            await_recv(grads.at[head], e_recv.at[head])
    for n in range(7):
        await_send(send.at[n], x_send.at[n])
        await_send(slot_send, sl_send.at[n])
        await_send(grads.at[0], a_send.at[n])
    for k in range(3):
        await_send(got_y.at[k], b_send.at[k])
        await_send(got_y.at[k], d_send.at[k])
    for offset in range(SIDE):
        for sem in (cp_send, cm_send, h_send, gm_send, gp_send):
            await_send(got_m.at[offset], sem.at[offset])

    for index, (_, parts) in enumerate(PASSED):
        await_send(kv.at[0, 0, parts], f_send.at[index])

    def sent_back(index):
        await_send(back.at[0], r_send.at[index])
        await_send(grads.at[0], e_send.at[index])

    for index in range(8):
        if index < 2:
            pl.when(c != index)(lambda: sent_back(index))
        else:
            sent_back(index)


def place_kernel(len_ref, prm_ref, *refs):
    blocks, (grads, attn, query, key, value, prefix_key, prefix_value) = refs[:BATCH], refs[BATCH:]
    step = pl.program_id(0)
    token = lax.broadcasted_iota(jnp.int32, (SLOTS, GW), 0)
    for m, block in enumerate(blocks):
        live = token < len_ref[step * BATCH + m]
        rows = slice(m * SLOTS, (m + 1) * SLOTS)
        for h in range(KEY_HEADS):
            attn[rows, h * GW : (h + 1) * GW] = jnp.where(live, block[h, 0, :, :GW], jnp.zeros((), BF16))
            query[rows, h * GW : (h + 1) * GW] = block[h, 0, :, GW : 2 * GW]
            key[rows, h * WIDTH : (h + 1) * WIDTH] = block[h, 0, :, 2 * GW : 2 * GW + WIDTH]
            value[rows, h * WIDTH : (h + 1) * WIDTH] = block[h, 0, :, 2 * GW + WIDTH :]

    @pl.when(step == 0)
    def _():
        for h in range(KEY_HEADS):
            prefix_key[:, h * WIDTH : (h + 1) * WIDTH] = grads[h, 0].astype(F32)
            prefix_value[:, h * WIDTH : (h + 1) * WIDTH] = grads[h, 1].astype(F32)


def spec(space):
    return pl.BlockSpec(memory_space=space)


DMA = pltpu.SemaphoreType.DMA


def local(queries, grad_out, response_keys, response_values, prompt_prefix_keys, prompt_prefix_values, lengths, prompt_of):
    q, g = queries.reshape(TOKENS, KEY_HEADS * GW), grad_out.reshape(TOKENS, KEY_HEADS * GW)
    k, v = response_keys.reshape(TOKENS, KEY_HEADS * WIDTH), response_values.reshape(TOKENS, KEY_HEADS * WIDTH)
    pk, pv = prompt_prefix_keys.reshape(ROWS, KEY_HEADS * WIDTH), prompt_prefix_values.reshape(ROWS, KEY_HEADS * WIDTH)
    lens, prompts = lengths.reshape(RESPONSES), prompt_of.reshape(RESPONSES)
    vmem = pltpu.VMEM
    back, grads = pl.pallas_call(
        main_kernel,
        out_shape=(
            jax.ShapeDtypeStruct((8, SIDE, SIDE * SLOTS, MSG), BF16),
            jax.ShapeDtypeStruct((8, 2, ROWS, WIDTH), BF16),
        ),
        in_specs=[spec(pltpu.SMEM)] * 2 + [spec(pl.ANY)] * 6,
        out_specs=(spec(pl.ANY),) * 2,
        scratch_shapes=[
            vmem((8, TOKENS, MSG), BF16), vmem((7, LIVE, MSG), BF16), vmem((8, LIVE), F32),
            vmem((8, LIVE, MSG), BF16), vmem((8, 8, LIVE), F32), vmem((SIDE, SIDE, SIDE, 2, 96, WIDTH), BF16),
            vmem((KEY_HEADS, 2, ROWS, WIDTH), BF16),
            vmem((RESPONSES, 8 * SLOTS, MSG), BF16), vmem((8, SIDE, SIDE * SLOTS, MSG), BF16),
            vmem((SIDE, SIDE, 2, PREFIX, WIDTH), BF16), vmem((SIDE, 2, PREFIX, WIDTH), BF16), vmem((SIDE, 2, PREFIX, WIDTH), BF16),
            vmem((SIDE, 2, PREFIX, WIDTH), BF16), vmem((SIDE, 2, PREFIX, WIDTH), BF16),
            vmem((3, 2, PREFIX, WIDTH), BF16), vmem((3, SIDE, 2, 96, WIDTH), BF16),
            vmem((2, PREFIX, WIDTH), BF16), vmem((SIDE, 2, 96, WIDTH), BF16),
            DMA((8,)), DMA((8,)), DMA((8,)), DMA((8,)), DMA((8,)), DMA((8,)), DMA((8,)), DMA((3,)), DMA((3,)),
        ] + [DMA((SIDE,))] * 4 + [DMA((6,))] * 2 + [DMA((SIDE,))] * 6 + [DMA((3,)), DMA((3,)), DMA((8,)), DMA((8,)), DMA((8,)), DMA((8,)), DMA((4,))],
        compiler_params=pltpu.CompilerParams(collective_id=0, has_side_effects=True, vmem_limit_bytes=VMEM_LIMIT),
    )(lens, prompts, q, g, k, v, pk, pv)
    def block_of(m):
        def index(i, lens, prompts):
            there = prompts[i * BATCH + m]
            return 0, there % SIDE, there // SIDE, 0

        return pl.BlockSpec((KEY_HEADS, 1, SLOTS, MSG), index)

    wide = pl.BlockSpec((BATCH * SLOTS, KEY_HEADS * GW), lambda i, *_: (i, 0))
    narrow = pl.BlockSpec((BATCH * SLOTS, KEY_HEADS * WIDTH), lambda i, *_: (i, 0))
    prefix = pl.BlockSpec((ROWS, KEY_HEADS * WIDTH), lambda i, *_: (0, 0))
    outs = pl.pallas_call(
        place_kernel,
        grid_spec=pltpu.PrefetchScalarGridSpec(
            num_scalar_prefetch=2,
            grid=(RESPONSES // BATCH,),
            in_specs=[block_of(m) for m in range(BATCH)] + [pl.BlockSpec(grads.shape, lambda i, *_: (0, 0, 0, 0))],
            out_specs=[wide, wide, narrow, narrow, prefix, prefix],
        ),
        out_shape=[
            jax.ShapeDtypeStruct(q.shape, BF16),
            jax.ShapeDtypeStruct(q.shape, BF16),
            jax.ShapeDtypeStruct(k.shape, BF16),
            jax.ShapeDtypeStruct(k.shape, BF16),
            jax.ShapeDtypeStruct(pk.shape, F32),
            jax.ShapeDtypeStruct(pk.shape, F32),
        ],
        compiler_params=pltpu.CompilerParams(vmem_limit_bytes=VMEM_LIMIT),
    )(lens, prompts, *[back] * BATCH, grads)
    shapes = (queries, queries, response_keys, response_keys, prompt_prefix_keys, prompt_prefix_keys)
    return tuple(out.reshape(like.shape) for out, like in zip(outs, shapes))


def solution(mesh):
    five, three = P("prompt", "resp", None, None, None), P("prompt", "resp", None)
    return jax.shard_map(
        local,
        mesh=mesh,
        in_specs=(five, five, five, five, three, three, three, three),
        out_specs=(five, five, five, five, three, three),
        check_vma=False,
    )
```

```python
import jax
import jax.numpy as jnp
from jax import lax
from jax.experimental import pallas as pl
from jax.experimental.pallas import tpu as pltpu
from jax.sharding import PartitionSpec as P

KEY_HEADS = 8
WIDTH = 128
GROUP = 5
SLOTS = 16
RESPONSES = 16
TOKENS = SLOTS * RESPONSES
LIVE = 160
PREFIX = 384
SIDE = 4
ROWS = PREFIX // 8
GW = GROUP * WIDTH
MSG = 2 * GW + 2 * WIDTH
MESH = pl.DeviceIdType.MESH
BF16 = jnp.bfloat16
F32 = jnp.float32
SCALE = WIDTH**-0.5
EXP2_SCALE = SCALE * 1.4426950408889634
BATCH = 8
HOLD = 14
FIRST = 2
LOW, HIGH, BOTH = pl.ds(0, 2), pl.ds(2, 2), pl.ds(0, 4)
PASSED = ((0, LOW), (0, HIGH), (1, BOTH), (3, BOTH), (2, LOW), (2, HIGH))
SHIFT = 0
VMEM_LIMIT = 58 * 1024 * 1024


class Place:
    def __init__(self):
        prompt, resp = lax.axis_index("prompt"), lax.axis_index("resp")
        self.y, self.z = prompt // SIDE, prompt % SIDE
        self.x, self.c = resp // 2, resp % 2
        self.prompt, self.resp = prompt, resp
        x, y, z, c = self.x, self.y, self.z, self.c
        self.sibling = (prompt, x * 2 + 1 - c)
        self.home_slot = 2 * (x * (1 - c) + y * c) + c
        self.head = x * (1 - c) + (SIDE + y) * c
        self.line = y * (1 - c) + x * c
        self.routes = []
        for k in (2, 1, 3):
            xd, yd = (x + k) % SIDE, (y + k) % SIDE
            self.routes.append((xd, 2 * x + c, (prompt, 2 * xd)))
            self.routes.append((SIDE + yd, 2 * y + c, (yd * SIDE + z, 2 * x + 1)))
        self.routes.append(((SIDE + y) * (1 - c) + x * c, 2 * y * (1 - c) + (2 * x + 1) * c, self.sibling))
        self.routes.append((self.head, self.home_slot, None))

    def source(self, k, core):
        along = (self.x * (1 - self.c) + self.y * self.c + k) % SIDE
        prompt = self.prompt * (1 - self.c) + (along * SIDE + self.z) * self.c
        resp = (along * 2 + core) * (1 - self.c) + (2 * self.x + core) * self.c
        return 2 * along + core, (prompt, resp)

    def line_peer(self, k):
        prompt = ((self.y + k * (1 - self.c)) % SIDE) * SIDE + self.z
        return (prompt, ((self.x + k * self.c) % SIDE) * 2 + self.c)

    def beside(self, n, k):
        x, y, z, c = self.x, self.y, self.z, self.c
        if n == 7:
            return self.line_peer(k)
        if n == 6:
            return (((y + k * c) % SIDE) * SIDE + z, ((x + k * (1 - c)) % SIDE) * 2 + 1 - c)
        ahead = (2, 1, 3)[n // 2]
        if n % 2 == 0:
            return (((y + k) % SIDE) * SIDE + z, 2 * ((x + ahead) % SIDE))
        return (((y + ahead) % SIDE) * SIDE + z, 2 * ((x + k) % SIDE) + 1)

    def z_peer(self, k):
        return (self.y * SIDE + (self.z + k) % SIDE, self.resp)

    def barrier(self):
        sem = pltpu.get_barrier_semaphore()
        peers = [self.sibling]
        for k in (1, 2, 3):
            peers.append(self.z_peer(k))
            for core in (0, 1):
                peers.append((self.prompt, ((self.x + k) % SIDE) * 2 + core))
                peers.append((((self.y + k) % SIDE) * SIDE + self.z, 2 * self.x + core))
                for j in (1, 2, 3):
                    peers.append((((self.y + k) % SIDE) * SIDE + self.z, ((self.x + j) % SIDE) * 2 + core))
        for peer in peers:
            pl.semaphore_signal(sem, inc=1, device_id=peer, device_id_type=MESH)
        pl.semaphore_wait(sem, len(peers))


def remote(src, dst, send, recv, device):
    return pltpu.make_async_remote_copy(
        src_ref=src, dst_ref=dst, send_sem=send, recv_sem=recv, device_id=device, device_id_type=MESH
    )


def pack_rows(len_ref, prm_ref):
    lane = lax.broadcasted_iota(jnp.int32, (1, TOKENS), 1)
    response, token = lane >> 4, lane & (SLOTS - 1)
    row = jnp.full((1, TOKENS), -1, jnp.int32)
    slot = jnp.zeros((1, TOKENS), jnp.int32)
    start = jnp.int32(0)
    for j in range(RESPONSES):
        length = len_ref[j]
        mine = response == j
        row = jnp.where(mine & (token < length), start + token, row)
        slot = jnp.where(mine, prm_ref[j] * SLOTS + token, slot)
        start = start + length
    return row, slot


def one_hot_pack(row):
    packed = lax.broadcasted_iota(jnp.int32, (LIVE, TOKENS), 0)
    return jnp.where(packed == row, 1.0, 0.0).astype(BF16)


def dot(a, b, dims):
    return lax.dot_general(a, b, (dims, ((), ())), preferred_element_type=F32)


NN = ((1,), (0,))
NT = ((1,), (1,))
TN = ((0,), (0,))


def main_kernel(
    len_ref, prm_ref, q, g, k, v, pk, pv, back, grads,
    xb, send, slot_send, recv, slots, kv, pkv, xu, ou, dkv, half_sum, got_m, got_p, plane_sum, got_y, got_x, final_y, final_x,
    in_sem, x_send, x_recv, sl_send, sl_recv, a_send, a_recv, b_send, b_recv,
    cp_send, cp_recv, cm_send, cm_recv, f_send, f_recv,
    h_send, h_recv, gm_send, gm_recv, gp_send, gp_recv, d_send, d_recv, e_send, e_recv, r_send, r_recv, own_sem,
):
    me = Place()
    routes = me.routes
    after, before = me.z_peer(1), me.z_peer(SIDE - 1)
    plane_of = lambda k: (me.z + k) % SIDE
    piece_of = lambda offset: (me.line + offset) % SIDE

    def core_rows(core):
        return pl.ds(pl.multiple_of(core * ROWS, 16), ROWS)

    def await_recv(ref, sem):
        remote(ref, ref, x_send.at[0], sem, me.sibling).wait_recv()

    def await_send(ref, sem):
        remote(ref, ref, sem, x_recv.at[0], me.sibling).wait_send()

    for n, (head, _, _) in enumerate(routes):
        wide = pl.ds(pl.multiple_of(head * GW, WIDTH), GW)
        narrow = pl.ds(pl.multiple_of(head * WIDTH, WIDTH), WIDTH)
        for src, cols, low, size in ((q, wide, 0, GW), (g, wide, GW, GW), (k, narrow, 2 * GW, WIDTH), (v, narrow, 2 * GW + WIDTH, WIDTH)):
            pltpu.make_async_copy(src.at[:, cols], xb.at[n, :, pl.ds(low, size)], in_sem.at[n]).start()
    for i, src in enumerate((pk, pv)):
        for h in range(KEY_HEADS):
            pltpu.make_async_copy(src.at[:, pl.ds(h * WIDTH, WIDTH)], pkv.at[h, i], own_sem.at[2]).start()
    me.barrier()
    pltpu.make_async_copy(pkv, pkv, own_sem.at[2]).wait()

    for k in (0, 1, 3):
        for n, (head, there, device) in enumerate(routes):
            on_y = head // SIDE
            piece, part = me.y * (1 - on_y) + me.x * on_y, me.x * (1 - on_y) + me.y * on_y
            src, dst = pkv.at[head], kv.at[me.z, piece, part, :, core_rows(me.c)]
            if k > 0:
                remote(src, dst, b_send.at[k - 1], b_recv.at[k - 1], me.beside(n, k)).start()
            elif device is None:
                pltpu.make_async_copy(src, dst, own_sem.at[1]).start()
            else:
                remote(src, dst, a_send.at[n], a_recv.at[there], device).start()

    row, slot = pack_rows(len_ref, prm_ref)
    pack = one_hot_pack(row)
    slot8 = jnp.broadcast_to(slot, (8, TOKENS)).astype(F32).astype(BF16)
    slot_send[...] = dot(slot8, pack, NT)
    for n, (_, there, device) in enumerate(routes):
        if device is None:
            pltpu.make_async_copy(slot_send, slots.at[there], own_sem.at[3]).start()
        else:
            remote(slot_send, slots.at[there], sl_send.at[n], sl_recv.at[there], device).start()

    def pack_rows_of(n):
        _, there, device = routes[n]
        pltpu.make_async_copy(xb.at[n], xb.at[n], in_sem.at[n]).wait()
        rows = dot(pack, xb[n], NN).astype(BF16)
        if device is None:
            recv[there] = rows
        else:
            send[n] = rows

    def send_rows(n):
        _, there, device = routes[n]
        if device is not None:
            remote(send.at[n], recv.at[there], x_send.at[n], x_recv.at[there], device).start()

    def pass_on(offset, index, parts, forward):
        ref = kv.at[plane_of(3 if forward else 1), piece_of(offset)]
        await_recv(ref, (cp_recv if forward else cm_recv).at[offset])
        ref = ref.at[parts]
        remote(ref, ref, f_send.at[index], f_recv.at[index], after if forward else before).start()

    def spread(offset):
        ref = kv.at[me.z, piece_of(offset)]
        remote(ref, ref, cp_send.at[offset], cp_recv.at[offset], after).start()
        remote(ref, ref, cm_send.at[offset], cm_recv.at[offset], before).start()

    for n in range(FIRST):
        pack_rows_of(n)
        send_rows(n)
    for k in range(SIDE):
        for core in (0, 1):
            there, _ = me.source(k, core)
            dst = kv.at[me.z, me.line, there // 2, :, core_rows(core)]
            if k == 0:
                pl.when(me.c == core)(lambda dst=dst: pltpu.make_async_copy(dst, dst, own_sem.at[1]).wait())
                pl.when(me.c != core)(lambda dst=dst, there=there: await_recv(dst, a_recv.at[there]))
            else:
                await_recv(dst, a_recv.at[there])
    ref = kv.at[me.z, me.line]
    remote(ref, ref, b_send.at[1], b_recv.at[1], me.line_peer(2)).start()
    spread(0)
    for n in range(FIRST, 4):
        pack_rows_of(n)
        send_rows(n)
    pass_on(0, 0, LOW, True)
    pass_on(0, 1, HIGH, False)
    for k in (1, 3, 2):
        await_recv(kv.at[me.z, piece_of(k)], b_recv.at[SIDE - k - 1])
        spread(k)
        n = {1: 4, 3: 5, 2: 6}[k]
        pack_rows_of(n)
        send_rows(n)
    pack_rows_of(7)
    pass_on(1, 2, BOTH, True)
    pass_on(3, 3, BOTH, False)
    pass_on(2, 4, LOW, True)
    pass_on(2, 5, HIGH, False)

    def one_hot(i):
        slot = slots[i][0:1].astype(jnp.int32)
        return jnp.where(lax.broadcasted_iota(jnp.int32, (TOKENS, LIVE), 0) == slot, 1.0, 0.0).astype(BF16)

    pltpu.make_async_copy(slot_send, slots.at[me.home_slot], own_sem.at[3]).wait()

    def unpack(m, carry):
        ahead = 2 + m // 2 + m // 4 + 2 * (m // 6)
        there = 2 * ((me.home_slot // 2 + ahead) % SIDE) + m % 2

        @pl.when(there != me.home_slot)
        def _():
            await_recv(slots.at[there], sl_recv.at[there])
            await_recv(recv.at[there], x_recv.at[there])

        rows = dot(one_hot(there), recv[there], NN).astype(BF16)
        xu[:, pl.ds(pl.multiple_of(there * SLOTS, SLOTS), SLOTS), :] = rows.reshape(RESPONSES, SLOTS, MSG)
        return carry

    lax.fori_loop(0, 8, unpack, 0)
    own_rows = lax.broadcasted_iota(jnp.int32, (WIDTH, WIDTH), 0)
    own_cols = lax.broadcasted_iota(jnp.int32, (WIDTH, WIDTH), 1)
    own_mask = (own_rows >> 4 == own_cols >> 4) & (own_cols <= own_rows)
    own_mask = jnp.concatenate([own_mask] * GROUP, axis=0)
    c = me.c

    def prompt(gz, gy):
        number = gy * SIDE + gz

        def chunk(i, quarter):
            return gz, gy * (1 - c) + quarter * c, quarter * (1 - c) + gy * c, i

        def heads(low):
            return jnp.concatenate([xu[number, :, low + a * WIDTH : low + (a + 1) * WIDTH] for a in range(GROUP)], axis=0)

        def put(low, rows):
            ou[:, gz, pl.ds(pl.multiple_of(gy * SLOTS, SLOTS), SLOTS), low : low + WIDTH] = rows.reshape(8, SLOTS, WIDTH)

        queries, grad_rows = heads(0), heads(GW)
        keys = jnp.concatenate([kv[chunk(0, i)] for i in range(SIDE)] + [xu[number, :, 2 * GW : 2 * GW + WIDTH]], axis=0)
        values = jnp.concatenate([kv[chunk(1, i)] for i in range(SIDE)] + [xu[number, :, 2 * GW + WIDTH :]], axis=0)
        scores = dot(queries, keys, NT)
        scores = jnp.concatenate([scores[:, :PREFIX], jnp.where(own_mask, scores[:, PREFIX:], -1e30)], axis=1)
        top = jnp.max(scores, axis=1, keepdims=True)
        weights = jnp.exp2((scores - top) * EXP2_SCALE)
        over = 1.0 / jnp.sum(weights, axis=1, keepdims=True)
        half = weights.astype(BF16)
        out = dot(half, values, NN) * over
        scaled = (grad_rows.astype(F32) * over).astype(BF16)
        row_dot = jnp.sum(scaled.astype(F32) * out, axis=1, keepdims=True)
        score_grad = (weights * (dot(scaled, values, NT) - row_dot)).astype(BF16)
        query_grad = dot(score_grad, keys, NN) * SCALE
        key_grad = (dot(score_grad, queries, TN) * SCALE).astype(BF16)
        value_grad = dot(half, scaled, TN).astype(BF16)
        dkv[gz, gy, 0] = key_grad[:PREFIX]
        dkv[gz, gy, 1] = value_grad[:PREFIX]
        for a in range(GROUP):
            put(a * WIDTH, out[a * WIDTH : (a + 1) * WIDTH].astype(BF16))
            put(GW + a * WIDTH, query_grad[a * WIDTH : (a + 1) * WIDTH].astype(BF16))
        put(2 * GW, key_grad[PREFIX:])
        put(2 * GW + WIDTH, value_grad[PREFIX:])

    def send_back(gz, gy):
        rows = pl.ds(pl.multiple_of(gy * SLOTS, SLOTS), SLOTS)
        for k in (2, 1, 3, 0):
            for core in (0, 1):
                there, device = me.source(k, core)
                index = 2 * k + core
                src, dst = ou.at[there, gz, rows], back.at[me.head, gz, rows]
                away = lambda: remote(src, dst, r_send.at[index], r_recv.at[me.head], device).start()
                if k == 0:
                    pl.when(c == core)(lambda: pltpu.make_async_copy(src, dst, own_sem.at[0]).start())
                    pl.when(c != core)(away)
                else:
                    away()

    def plan(n):
        quarter, odd = n // 4, n % 2
        first, middle = 1 - (quarter + 3) // 4, (quarter * (3 - quarter)) // 2
        ahead = first * 2 + middle * (1 + 2 * odd)
        gy = first * (odd * 2 + n // 2) + middle * (((n + 4) // 2 + 2 * (1 - odd)) % SIDE) + (1 - first - middle) * (n % SIDE)
        return (me.z + ahead) % SIDE, gy

    def step(count, carry):
        n = (count + SHIFT) % RESPONSES
        gz, gy = plan(n)

        @pl.when(n == 0)
        def _():
            for index, (offset, parts) in enumerate(PASSED):
                await_recv(kv.at[plane_of(2), piece_of(offset), parts], f_recv.at[index])

        @pl.when(n == 4)
        def _():
            await_recv(kv.at[plane_of(1), piece_of(1)], cm_recv.at[1])
            await_recv(kv.at[plane_of(3), piece_of(3)], cp_recv.at[3])

        prompt(gz, gy)

        @pl.when((n >= 8) & (n < 12))
        def _():
            await_recv(half_sum.at[gy], h_recv.at[gy])
            dkv[gz, gy] = (dkv[gz, gy].astype(F32) + half_sum[gy].astype(F32)).astype(BF16)

        for odd, device, got, send_sem, recv_sem in ((0, after, got_m, gm_send, gm_recv), (1, before, got_p, gp_send, gp_recv)):

            @pl.when((n < 4) & (n % 2 == odd))
            def _():
                remote(dkv.at[gz, gy], half_sum.at[gy], h_send.at[gy], h_recv.at[gy], device).start()

            @pl.when((n >= 4) & (n < 12) & (n % 2 == odd))
            def _():
                remote(dkv.at[gz, gy], got.at[gy], send_sem.at[gy], recv_sem.at[gy], device).start()

        @pl.when(count < HOLD)
        def _():
            send_back(gz, gy)

        return carry

    lax.fori_loop(0, RESPONSES, step, 0)

    def add_up(gy, carry):
        await_recv(got_m.at[gy], gm_recv.at[gy])
        await_recv(got_p.at[gy], gp_recv.at[gy])
        total = dkv[me.z, gy].astype(F32) + got_m[gy].astype(F32) + got_p[gy].astype(F32)
        plane_sum[gy] = total.astype(BF16)
        return carry

    lax.fori_loop(0, SIDE, add_up, 0)

    def columns(k):
        return pl.ds(pl.multiple_of((me.x + k) % SIDE * 96, 16), 96)

    @pl.when(c == 0)
    def _():
        for k in (2, 1, 3):
            remote(plane_sum.at[(me.y + k) % SIDE], got_y.at[k - 1], d_send.at[k - 1], d_recv.at[k - 1], me.line_peer(k)).start()

    @pl.when(c != 0)
    def _():
        for k in (2, 1, 3):
            remote(plane_sum.at[:, :, columns(k)], got_x.at[k - 1], d_send.at[k - 1], d_recv.at[k - 1], me.line_peer(k)).start()

    def late(n, carry):
        send_back(*plan((n + SHIFT) % RESPONSES))
        return carry

    lax.fori_loop(HOLD, RESPONSES, late, 0)

    def send_grads(part):
        for k in (2, 1, 3, 0):
            for core in (0, 1):
                _, device = me.source(k, core)
                index = 2 * k + core
                src, dst = part(k, core), grads.at[me.head]
                if k > 0 or core == 1 - part.core:
                    remote(src, dst, e_send.at[index], e_recv.at[me.head], device).start()
                else:
                    pltpu.make_async_copy(src, dst, own_sem.at[1]).start()

    @pl.when(c == 0)
    def _():
        total = plane_sum[me.y].astype(F32)
        for k in (1, 3, 2):
            await_recv(got_y.at[k - 1], d_recv.at[k - 1])
            total = total + got_y[k - 1].astype(F32)
        final_y[...] = total.astype(BF16)

        def part(k, core):
            return final_y.at[:, pl.ds(pl.multiple_of((2 * ((me.x + k) % SIDE) + core) * ROWS, 16), ROWS)]

        part.core = 0
        send_grads(part)

    @pl.when(c != 0)
    def _():
        total = plane_sum[:, :, columns(0)].astype(F32)
        for k in (1, 3, 2):
            await_recv(got_x.at[k - 1], d_recv.at[k - 1])
            total = total + got_x[k - 1].astype(F32)
        final_x[...] = total.astype(BF16)

        def part(k, core):
            return final_x.at[(me.y + k) % SIDE, :, pl.ds(core * ROWS, ROWS)]

        part.core = 1
        send_grads(part)

    for head, _, device in routes:
        if device is None:
            pltpu.make_async_copy(back.at[head], back.at[head], own_sem.at[0]).wait()
            pltpu.make_async_copy(grads.at[head], grads.at[head], own_sem.at[1]).wait()
        else:
            await_recv(back.at[head], r_recv.at[head])
            await_recv(grads.at[head], e_recv.at[head])
    for n in range(7):
        await_send(send.at[n], x_send.at[n])
        await_send(slot_send, sl_send.at[n])
        await_send(grads.at[0], a_send.at[n])
    for k in range(3):
        await_send(got_y.at[k], b_send.at[k])
        await_send(got_y.at[k], d_send.at[k])
    for offset in range(SIDE):
        for sem in (cp_send, cm_send, h_send, gm_send, gp_send):
            await_send(got_m.at[offset], sem.at[offset])

    for index, (_, parts) in enumerate(PASSED):
        await_send(kv.at[0, 0, parts], f_send.at[index])

    def sent_back(index):
        await_send(back.at[0], r_send.at[index])
        await_send(grads.at[0], e_send.at[index])

    for index in range(8):
        if index < 2:
            pl.when(c != index)(lambda: sent_back(index))
        else:
            sent_back(index)


def place_kernel(len_ref, prm_ref, *refs):
    blocks, (grads, attn, query, key, value, prefix_key, prefix_value) = refs[:BATCH], refs[BATCH:]
    step = pl.program_id(0)
    token = lax.broadcasted_iota(jnp.int32, (SLOTS, GW), 0)
    for m, block in enumerate(blocks):
        live = token < len_ref[step * BATCH + m]
        rows = slice(m * SLOTS, (m + 1) * SLOTS)
        for h in range(KEY_HEADS):
            attn[rows, h * GW : (h + 1) * GW] = jnp.where(live, block[h, 0, :, :GW], jnp.zeros((), BF16))
            query[rows, h * GW : (h + 1) * GW] = block[h, 0, :, GW : 2 * GW]
            key[rows, h * WIDTH : (h + 1) * WIDTH] = block[h, 0, :, 2 * GW : 2 * GW + WIDTH]
            value[rows, h * WIDTH : (h + 1) * WIDTH] = block[h, 0, :, 2 * GW + WIDTH :]

    @pl.when(step == 0)
    def _():
        for h in range(KEY_HEADS):
            prefix_key[:, h * WIDTH : (h + 1) * WIDTH] = grads[h, 0].astype(F32)
            prefix_value[:, h * WIDTH : (h + 1) * WIDTH] = grads[h, 1].astype(F32)


def spec(space):
    return pl.BlockSpec(memory_space=space)


DMA = pltpu.SemaphoreType.DMA


def local(queries, grad_out, response_keys, response_values, prompt_prefix_keys, prompt_prefix_values, lengths, prompt_of):
    q, g = queries.reshape(TOKENS, KEY_HEADS * GW), grad_out.reshape(TOKENS, KEY_HEADS * GW)
    k, v = response_keys.reshape(TOKENS, KEY_HEADS * WIDTH), response_values.reshape(TOKENS, KEY_HEADS * WIDTH)
    pk, pv = prompt_prefix_keys.reshape(ROWS, KEY_HEADS * WIDTH), prompt_prefix_values.reshape(ROWS, KEY_HEADS * WIDTH)
    lens, prompts = lengths.reshape(RESPONSES), prompt_of.reshape(RESPONSES)
    vmem = pltpu.VMEM
    back, grads = pl.pallas_call(
        main_kernel,
        out_shape=(
            jax.ShapeDtypeStruct((8, SIDE, SIDE * SLOTS, MSG), BF16),
            jax.ShapeDtypeStruct((8, 2, ROWS, WIDTH), BF16),
        ),
        in_specs=[spec(pltpu.SMEM)] * 2 + [spec(pl.ANY)] * 6,
        out_specs=(spec(pl.ANY),) * 2,
        scratch_shapes=[
            vmem((8, TOKENS, MSG), BF16), vmem((7, LIVE, MSG), BF16), vmem((8, LIVE), F32),
            vmem((8, LIVE, MSG), BF16), vmem((8, 8, LIVE), F32), vmem((SIDE, SIDE, SIDE, 2, 96, WIDTH), BF16),
            vmem((KEY_HEADS, 2, ROWS, WIDTH), BF16),
            vmem((RESPONSES, 8 * SLOTS, MSG), BF16), vmem((8, SIDE, SIDE * SLOTS, MSG), BF16),
            vmem((SIDE, SIDE, 2, PREFIX, WIDTH), BF16), vmem((SIDE, 2, PREFIX, WIDTH), BF16), vmem((SIDE, 2, PREFIX, WIDTH), BF16),
            vmem((SIDE, 2, PREFIX, WIDTH), BF16), vmem((SIDE, 2, PREFIX, WIDTH), BF16),
            vmem((3, 2, PREFIX, WIDTH), BF16), vmem((3, SIDE, 2, 96, WIDTH), BF16),
            vmem((2, PREFIX, WIDTH), BF16), vmem((SIDE, 2, 96, WIDTH), BF16),
            DMA((8,)), DMA((8,)), DMA((8,)), DMA((8,)), DMA((8,)), DMA((8,)), DMA((8,)), DMA((3,)), DMA((3,)),
        ] + [DMA((SIDE,))] * 4 + [DMA((6,))] * 2 + [DMA((SIDE,))] * 6 + [DMA((3,)), DMA((3,)), DMA((8,)), DMA((8,)), DMA((8,)), DMA((8,)), DMA((4,))],
        compiler_params=pltpu.CompilerParams(collective_id=0, has_side_effects=True, vmem_limit_bytes=VMEM_LIMIT),
    )(lens, prompts, q, g, k, v, pk, pv)
    def block_of(m):
        def index(i, lens, prompts):
            there = prompts[i * BATCH + m]
            return 0, there % SIDE, there // SIDE, 0

        return pl.BlockSpec((KEY_HEADS, 1, SLOTS, MSG), index)

    wide = pl.BlockSpec((BATCH * SLOTS, KEY_HEADS * GW), lambda i, *_: (i, 0))
    narrow = pl.BlockSpec((BATCH * SLOTS, KEY_HEADS * WIDTH), lambda i, *_: (i, 0))
    prefix = pl.BlockSpec((ROWS, KEY_HEADS * WIDTH), lambda i, *_: (0, 0))
    outs = pl.pallas_call(
        place_kernel,
        grid_spec=pltpu.PrefetchScalarGridSpec(
            num_scalar_prefetch=2,
            grid=(RESPONSES // BATCH,),
            in_specs=[block_of(m) for m in range(BATCH)] + [pl.BlockSpec(grads.shape, lambda i, *_: (0, 0, 0, 0))],
            out_specs=[wide, wide, narrow, narrow, prefix, prefix],
        ),
        out_shape=[
            jax.ShapeDtypeStruct(q.shape, BF16),
            jax.ShapeDtypeStruct(q.shape, BF16),
            jax.ShapeDtypeStruct(k.shape, BF16),
            jax.ShapeDtypeStruct(k.shape, BF16),
            jax.ShapeDtypeStruct(pk.shape, F32),
            jax.ShapeDtypeStruct(pk.shape, F32),
        ],
        compiler_params=pltpu.CompilerParams(vmem_limit_bytes=VMEM_LIMIT),
    )(lens, prompts, *[back] * BATCH, grads)
    shapes = (queries, queries, response_keys, response_keys, prompt_prefix_keys, prompt_prefix_keys)
    return tuple(out.reshape(like.shape) for out, like in zip(outs, shapes))


def solution(mesh):
    five, three = P("prompt", "resp", None, None, None), P("prompt", "resp", None)
    return jax.shard_map(
        local,
        mesh=mesh,
        in_specs=(five, five, five, five, three, three, three, three),
        out_specs=(five, five, five, five, three, three),
        check_vma=False,
    )
```
